256 devices in a mesh: rows: 32 (over y_hi, z, core), pairs: 8 (over y_lo, x).
Axes of the slice: x: 4, y: 4 (y_hi: 2, y_lo: 2; y = y_hi * 2 + y_lo), z: 8, core: 2. Of those that a mesh axis runs over, the one named last changes fastest.
Arguments:
- loads: float32 [8192, 4096], P('rows', 'pairs'), may hold values from -6 to 6
- col_weights: float32 [4096], P('pairs'), may hold values from 0.3 to 3
- partner_offsets: int32 [2, 2], replicated, may hold values from 0 to 127
- skip_mask: int32 [2, 16], P(None, 'pairs'), may hold values 0 or 1
Outputs:
- rotated: float32 [8192, 4096], P('rows', 'pairs')
- column_power: float32 [4096], P('pairs')
The draws below stay inside these ranges and needn't reach their ends.
All inputs are finite; a program needn't handle non-finite values. No bound on the sum of `skip_mask` on one device may be relied on, other than what follows from the above.
Results may differ from the reference program's by a relative error of at most 0.0003.
Values sent between devices are 32-bit elements; how exact they have to be, the bound alone decides.
No kernel may reach another device: no remote copies, remote signals or barrier semaphores. Data moves between devices by JAX's collectives and lax.ppermute only.
A program may use at most 128 MiB of HBM per device.

```python
import math
import jax
import jax.numpy as jnp
from jax import lax

BLOCK = 128
STEPS = 2
INNER = 2
COLS = 4096
PAIRS = 16
PAIRS_DEV = 2
ROWS = 8192
N_PAIRS = 8


def place_ends(array, own_key, least, high):
    shape = array.shape
    spot = [jax.random.randint(jax.random.fold_in(own_key, axis), (), 0, shape[axis]) for axis in range(len(shape))]
    array = array.at[tuple(spot)].set(least)
    longest = shape.index(max(shape))
    spot[longest] = (spot[longest] + 1) % shape[longest]
    return array.at[tuple(spot)].set(high)


def block_scale(key, shape, cuts, smallest, high):
    level, own = 1.0, jax.random.fold_in(key, 6)
    for axis_at, blocks in cuts:
        steps = jnp.exp(jax.random.uniform(jax.random.fold_in(own, axis_at), (blocks,), jnp.float32, smallest / len(cuts), high / len(cuts)))
        level = level * jnp.repeat(steps, shape[axis_at] // blocks).reshape([-1 if axis == axis_at else 1 for axis in range(len(shape))])
    return level


def bell_draw(stream_key, extent, spread, reach, shards=(), held_as=jnp.bfloat16):
    entries = spread * jax.random.normal(stream_key, extent, jnp.float32)
    if shards:
        entries = entries * block_scale(stream_key, extent, shards, -0.22, 0.18)
    return jnp.clip(entries, -reach, reach).astype(held_as)


def setup_inputs(seed: int = 0) -> dict:
    key_list = jax.random.split(jax.random.key(seed), 5)
    loads = bell_draw(key_list[0], (ROWS, COLS), 1.0, 6.0, ((0, 32), (1, 8)), jnp.float32)
    col_weights = jnp.clip(jnp.exp(math.log(3.0) - 2.3025851 * jax.random.uniform(key_list[1], (COLS,), jnp.float32) ** block_scale(key_list[1], (COLS,), ((0, 8),), -0.2, 0.2)), 0.3, 3.0)
    partner_offsets = place_ends(jax.random.randint(key_list[2], (STEPS, INNER), 0, BLOCK), jax.random.fold_in(key_list[2], 1), 0, BLOCK - 1).astype(jnp.int32)
    skip_mask = place_ends((jax.random.randint(key_list[3], (STEPS, PAIRS), 0, 4) < 1).astype(jnp.int32), jax.random.fold_in(key_list[3], 1), 0, 1)
    return {"loads": loads, "col_weights": col_weights, "partner_offsets": partner_offsets, "skip_mask": skip_mask}


precise = lax.Precision.HIGHEST

def turn_columns(matrix, cosine_values, sine_values, offset):
    half_width = matrix.shape[-1] // 2
    left_part = matrix[..., :half_width]
    right_part = jnp.roll(matrix[..., half_width:], -offset, axis=-1)
    cosine_grid = cosine_values[:, None, :]
    sine_grid = sine_values[:, None, :]
    new_left = cosine_grid * left_part - sine_grid * right_part
    new_right = jnp.roll(sine_grid * left_part + cosine_grid * right_part, offset, axis=-1)
    return jnp.concatenate([new_left, new_right], axis=-1)

def rotate_pair(gram_matrix, offsets_step, skip_step):
    half_width = gram_matrix.shape[-1] // 2
    identity = jnp.broadcast_to(jnp.eye(2 * half_width, dtype=jnp.float32), gram_matrix.shape)
    turned = gram_matrix
    rotation = identity
    for step_round in range(offsets_step.shape[0]):
        offset = offsets_step[step_round]
        diagonal_values = jnp.diagonal(turned, axis1=1, axis2=2)
        first_norms = diagonal_values[:, :half_width]
        second_norms = jnp.roll(diagonal_values[:, half_width:], -offset, axis=1)
        coupling = jnp.diagonal(jnp.roll(turned[:, :half_width, half_width:], -offset, axis=2), axis1=1, axis2=2)
        half_gap = 0.5 * (second_norms - first_norms)
        gap_sign = jnp.where(half_gap >= 0.0, 1.0, -1.0)
        denominator = jnp.maximum(jnp.abs(half_gap) + jnp.sqrt(half_gap * half_gap + coupling * coupling), 1e-06 * (first_norms + second_norms))
        tangent = gap_sign * coupling / denominator
        cosine_values = 1.0 / jnp.sqrt(1.0 + tangent * tangent)
        sine_values = tangent * cosine_values
        turned = turn_columns(turned, cosine_values, sine_values, offset)
        turned = jnp.swapaxes(turn_columns(jnp.swapaxes(turned, 1, 2), cosine_values, sine_values, offset), 1, 2)
        rotation = turn_columns(rotation, cosine_values, sine_values, offset)
    unskipped = (skip_step == 0)[:, None, None]
    return (jnp.where(unskipped, rotation, identity), jnp.where(unskipped, turned, gram_matrix))

def reference(loads, col_weights, partner_offsets, skip_mask):
    weighted = loads * col_weights[None, :]
    blocks = weighted.reshape(ROWS, N_PAIRS, 2, PAIRS_DEV, BLOCK).transpose(2, 1, 3, 0, 4).reshape(2, PAIRS, ROWS, BLOCK)
    upper_blocks = blocks[0]
    lower_blocks = blocks[1]
    for step_index in range(STEPS):
        joined = jnp.concatenate([upper_blocks, lower_blocks], axis=-1)
        gram_matrix = jnp.einsum('prc,prd->pcd', joined, joined, precision=precise, preferred_element_type=jnp.float32)
        rotation, turned = rotate_pair(gram_matrix, partner_offsets[step_index], skip_mask[step_index])
        joined = jnp.einsum('prc,pcd->prd', joined, rotation, precision=precise, preferred_element_type=jnp.float32)
        upper_blocks = joined[..., :BLOCK]
        lower_blocks = joined[..., BLOCK:]
        if step_index + 1 < STEPS:
            new_upper = jnp.concatenate([upper_blocks[:1], lower_blocks[:1], upper_blocks[1:-1]], axis=0)
            new_lower = jnp.concatenate([lower_blocks[1:], upper_blocks[-1:]], axis=0)
            upper_blocks = new_upper
            lower_blocks = new_lower
    final_blocks = jnp.stack([upper_blocks, lower_blocks]).reshape(2, N_PAIRS, PAIRS_DEV, ROWS, BLOCK)
    rotated = final_blocks.transpose(3, 1, 0, 2, 4).reshape(ROWS, COLS)
    column_power = lax.optimization_barrier(jnp.sum(rotated * rotated, axis=0)) / ROWS
    return (rotated, column_power)
```

```python
import functools
import jax
import jax.numpy as jnp
from jax import lax
from jax.experimental import pallas as pl
from jax.experimental.pallas import tpu as pltpu
from jax.sharding import PartitionSpec as P

BLOCK = 128
STEPS = 2
GROUP = 8

ENTRIES = 7
PADDED = 8


def left(x, by):
    return pltpu.roll(x, (BLOCK - by) & (BLOCK - 1), 1)


def right(x, by):
    return pltpu.roll(x, by, 1)


def pair_entries(load_pair, rows, first, second):
    gap = (second - first) & (BLOCK - 1)
    sums = [None] * ENTRIES
    for start in range(0, rows, GROUP):
        upper, lower = load_pair(start)
        lower_first = left(lower, first)
        lower_second = left(lower, second)
        upper_gap = left(upper, gap)
        terms = (
            upper * upper,
            lower * lower,
            upper * lower_first,
            upper * lower_second,
            upper_gap * lower_first,
            upper * upper_gap,
            lower_first * lower_second,
        )
        sums = [term if total is None else total + term for total, term in zip(sums, terms)]
    reduced = [jnp.sum(total, axis=0, keepdims=True) for total in sums]
    return jnp.concatenate(reduced + [jnp.zeros_like(reduced[0])], axis=0)


def angle(first_norms, second_norms, coupling):
    half_gap = 0.5 * (second_norms - first_norms)
    gap_sign = jnp.where(half_gap >= 0.0, 1.0, -1.0)
    denominator = jnp.maximum(
        jnp.abs(half_gap) + jnp.sqrt(half_gap * half_gap + coupling * coupling),
        1e-06 * (first_norms + second_norms),
    )
    tangent = gap_sign * coupling / denominator
    cosine = 1.0 / jnp.sqrt(1.0 + tangent * tangent)
    return cosine, tangent * cosine


def turned_norms(first_norms, second_norms, coupling, cosine, sine):
    new_first = cosine * (cosine * first_norms - sine * coupling) - sine * (cosine * coupling - sine * second_norms)
    new_second = sine * (sine * first_norms + cosine * coupling) + cosine * (sine * coupling + cosine * second_norms)
    return new_first, new_second


def pair_angles(entries, first, second, skip):
    gap = (second - first) & (BLOCK - 1)
    uu, ll, ul_first, ul_second, ul_gap, uu_gap, ll_gap = [entries[i : i + 1] for i in range(ENTRIES)]
    ll_first = left(ll, first)
    cosine, sine = angle(uu, ll_first, ul_first)
    upper_norms, lower_norms = turned_norms(uu, ll_first, ul_first, cosine, sine)
    cosine_gap = left(cosine, gap)
    sine_gap = left(sine, gap)
    coupling = cosine * (sine_gap * uu_gap + cosine_gap * ul_second) - sine * (sine_gap * ul_gap + cosine_gap * ll_gap)
    lower_norms = left(lower_norms, gap)
    cosine_last, sine_last = angle(upper_norms, lower_norms, coupling)
    upper_norms, lower_norms = turned_norms(upper_norms, lower_norms, coupling, cosine_last, sine_last)
    keep = skip != 0
    one, zero = jnp.ones_like(cosine), jnp.zeros_like(cosine)
    turns = (
        jnp.where(keep, one, cosine),
        jnp.where(keep, zero, sine),
        jnp.where(keep, one, cosine_last),
        jnp.where(keep, zero, sine_last),
    )
    return turns, jnp.where(keep, uu, upper_norms), jnp.where(keep, ll, right(lower_norms, second))


def turn(upper, lower, turns, first, second):
    gap = (second - first) & (BLOCK - 1)
    cosine, sine, cosine_last, sine_last = turns
    lower = left(lower, first)
    upper, lower = cosine * upper - sine * lower, sine * upper + cosine * lower
    lower = left(lower, gap)
    upper, lower = cosine_last * upper - sine_last * lower, sine_last * upper + cosine_last * lower
    return upper, right(lower, second)


def block_of(loads_ref, weights, block):
    columns = slice(block * BLOCK, (block + 1) * BLOCK)
    weight = weights[:, columns]
    return lambda start: loads_ref[start : start + GROUP, columns] * weight


def entries_kernel(offsets_ref, loads_ref, weights_ref, out_ref):
    rows = loads_ref.shape[0]
    weights = weights_ref[...]
    blocks = [block_of(loads_ref, weights, block) for block in range(4)]
    for pair in range(2):
        upper, lower = blocks[pair], blocks[2 + pair]
        out_ref[pair * PADDED : (pair + 1) * PADDED, :] = pair_entries(
            lambda start: (upper(start), lower(start)), rows, offsets_ref[0, 0], offsets_ref[0, 1]
        )


def first_turn_kernel(offsets_ref, skip_ref, place_ref, parts_ref, loads_ref, weights_ref,
                      even_ref, odd_ref, upper_ref, lower_ref):
    rows = loads_ref.shape[0]
    first, second = offsets_ref[0, 0], offsets_ref[0, 1]
    weights = weights_ref[...]
    blocks = [block_of(loads_ref, weights, block) for block in range(4)]
    total = parts_ref[0]
    for part in range(1, parts_ref.shape[0]):
        total = total + parts_ref[part]
    is_even = (place_ref[0] & 1) == 0
    turns = [
        pair_angles(total[pair * PADDED : (pair + 1) * PADDED], first, second, skip_ref[0, pair])[0]
        for pair in range(2)
    ]
    for start in range(0, rows, GROUP):
        span = slice(start, start + GROUP)
        upper_0, lower_0 = turn(blocks[0](start), blocks[2](start), turns[0], first, second)
        upper_1, lower_1 = turn(blocks[1](start), blocks[3](start), turns[1], first, second)
        upper_ref[span, :] = upper_0
        lower_ref[span, :] = lower_1
        even_ref[span, :] = jnp.where(is_even, upper_1, lower_0)
        odd_ref[span, :] = jnp.where(is_even, lower_0, upper_1)


def moved(place_ref, even_ref, odd_ref, upper_ref, lower_ref):
    is_even = (place_ref[0] & 1) == 0
    is_head = place_ref[0] == 0

    def load(start):
        span = slice(start, start + GROUP)
        even, odd, upper = even_ref[span, :], odd_ref[span, :], upper_ref[span, :]
        coming_upper = jnp.where(is_even, odd, even)
        coming_lower = jnp.where(is_even, even, odd)
        return (
            (jnp.where(is_head, upper, coming_upper), lower_ref[span, :]),
            (jnp.where(is_head, coming_upper, upper), coming_lower),
        )

    return load


def moved_entries_kernel(offsets_ref, place_ref, even_ref, odd_ref, upper_ref, lower_ref, out_ref):
    rows = even_ref.shape[0]
    load = moved(place_ref, even_ref, odd_ref, upper_ref, lower_ref)
    for pair in range(2):
        out_ref[pair * PADDED : (pair + 1) * PADDED, :] = pair_entries(
            lambda start: load(start)[pair], rows, offsets_ref[1, 0], offsets_ref[1, 1]
        )


def last_turn_kernel(total_rows, offsets_ref, skip_ref, place_ref, parts_ref, even_ref, odd_ref, upper_ref, lower_ref,
                     rotated_ref, power_ref):
    rows = even_ref.shape[0]
    first, second = offsets_ref[1, 0], offsets_ref[1, 1]
    load = moved(place_ref, even_ref, odd_ref, upper_ref, lower_ref)
    total = parts_ref[0]
    for part in range(1, parts_ref.shape[0]):
        total = total + parts_ref[part]
    turns = []
    for pair in range(2):
        own, upper_norms, lower_norms = pair_angles(
            total[pair * PADDED : (pair + 1) * PADDED], first, second, skip_ref[1, pair]
        )
        turns.append(own)
        power_ref[:, pair * BLOCK : (pair + 1) * BLOCK] = upper_norms / total_rows
        power_ref[:, (2 + pair) * BLOCK : (3 + pair) * BLOCK] = lower_norms / total_rows
    for start in range(0, rows, GROUP):
        span = slice(start, start + GROUP)
        for pair, (upper, lower) in enumerate(load(start)):
            upper, lower = turn(upper, lower, turns[pair], first, second)
            rotated_ref[span, pair * BLOCK : (pair + 1) * BLOCK] = upper
            rotated_ref[span, (2 + pair) * BLOCK : (3 + pair) * BLOCK] = lower


SMEM = pl.BlockSpec(memory_space=pltpu.SMEM)
VMEM = pl.BlockSpec(memory_space=pltpu.VMEM)


def call(kernel, scalars, arrays, shapes, name):
    several = isinstance(shapes, list)
    outs = [jax.ShapeDtypeStruct(shape, jnp.float32) for shape in (shapes if several else [shapes])]
    return pl.pallas_call(
        kernel,
        out_shape=outs if several else outs[0],
        in_specs=[SMEM] * len(scalars) + [VMEM] * len(arrays),
        out_specs=[VMEM] * len(outs) if several else VMEM,
        name=name,
    )(*scalars, *arrays)


def sum_parts(entries):
    size = lax.axis_size("rows")
    entries = entries + lax.ppermute(entries, "rows", [(row, row ^ 1) for row in range(size)])
    groups = [list(range(core, size, 2)) for core in range(2)]
    copies = jnp.broadcast_to(entries[None], (size // 2,) + entries.shape)
    return lax.all_to_all(copies, "rows", 0, 0, axis_index_groups=groups)


def per_device(loads, col_weights, partner_offsets, skip_mask):
    rows, columns = loads.shape
    pairs = lax.axis_size("pairs")
    place = lax.axis_index("pairs").reshape(1)
    weights = col_weights.reshape(1, columns)
    block = (rows, BLOCK)
    entries = call(entries_kernel, [partner_offsets], [loads, weights], (2 * PADDED, BLOCK), "entries")
    parts = sum_parts(entries)
    even, odd, upper, lower = call(
        first_turn_kernel, [partner_offsets, skip_mask, place], [parts, loads, weights], [block] * 4, "first_turn"
    )
    even = lax.ppermute(even, "pairs", [(at, at ^ 1) for at in range(pairs)])
    odd = lax.ppermute(odd, "pairs", [(at, min(max(((at + 1) ^ 1) - 1, 0), pairs - 1)) for at in range(pairs)])
    held = [even, odd, upper, lower]
    entries = call(moved_entries_kernel, [partner_offsets, place], held, (2 * PADDED, BLOCK), "moved_entries")
    parts = sum_parts(entries)
    total_rows = rows * lax.axis_size("rows")
    rotated, power = call(
        functools.partial(last_turn_kernel, float(total_rows)),
        [partner_offsets, skip_mask, place], [parts] + held, [(rows, columns), (1, columns)], "last_turn",
    )
    return rotated, power.reshape(columns)


def solution(mesh):
    in_specs = (P("rows", "pairs"), P("pairs"), P(), P(None, "pairs"))
    out_specs = (P("rows", "pairs"), P("pairs"))
    return jax.shard_map(
        per_device, mesh=mesh, in_specs=in_specs, out_specs=out_specs, check_vma=False
    )
```

```python
import functools
import jax
import jax.numpy as jnp
from jax import lax
from jax.experimental import pallas as pl
from jax.experimental.pallas import tpu as pltpu
from jax.sharding import PartitionSpec as P

BLOCK = 128
STEPS = 2
GROUP = 8

ENTRIES = 7
PADDED = 8


def left(x, by):
    return pltpu.roll(x, (BLOCK - by) & (BLOCK - 1), 1)


def right(x, by):
    return pltpu.roll(x, by, 1)


def pair_entries(load_pair, rows, first, second):
    gap = (second - first) & (BLOCK - 1)
    sums = [None] * ENTRIES
    for start in range(0, rows, GROUP):
        upper, lower = load_pair(start)
        lower_first = left(lower, first)
        lower_second = left(lower, second)
        upper_gap = left(upper, gap)
        terms = (
            upper * upper,
            lower * lower,
            upper * lower_first,
            upper * lower_second,
            upper_gap * lower_first,
            upper * upper_gap,
            lower_first * lower_second,
        )
        sums = [term if total is None else total + term for total, term in zip(sums, terms)]
    reduced = [jnp.sum(total, axis=0, keepdims=True) for total in sums]
    return jnp.concatenate(reduced + [jnp.zeros_like(reduced[0])], axis=0)


def angle(first_norms, second_norms, coupling):
    half_gap = 0.5 * (second_norms - first_norms)
    gap_sign = jnp.where(half_gap >= 0.0, 1.0, -1.0)
    denominator = jnp.maximum(
        jnp.abs(half_gap) + jnp.sqrt(half_gap * half_gap + coupling * coupling),
        1e-06 * (first_norms + second_norms),
    )
    tangent = gap_sign * coupling / denominator
    cosine = 1.0 / jnp.sqrt(1.0 + tangent * tangent)
    return cosine, tangent * cosine


def turned_norms(first_norms, second_norms, coupling, cosine, sine):
    new_first = cosine * (cosine * first_norms - sine * coupling) - sine * (cosine * coupling - sine * second_norms)
    new_second = sine * (sine * first_norms + cosine * coupling) + cosine * (sine * coupling + cosine * second_norms)
    return new_first, new_second


def pair_angles(entries, first, second, skip):
    gap = (second - first) & (BLOCK - 1)
    uu, ll, ul_first, ul_second, ul_gap, uu_gap, ll_gap = [entries[i : i + 1] for i in range(ENTRIES)]
    ll_first = left(ll, first)
    cosine, sine = angle(uu, ll_first, ul_first)
    upper_norms, lower_norms = turned_norms(uu, ll_first, ul_first, cosine, sine)
    cosine_gap = left(cosine, gap)
    sine_gap = left(sine, gap)
    coupling = cosine * (sine_gap * uu_gap + cosine_gap * ul_second) - sine * (sine_gap * ul_gap + cosine_gap * ll_gap)
    lower_norms = left(lower_norms, gap)
    cosine_last, sine_last = angle(upper_norms, lower_norms, coupling)
    upper_norms, lower_norms = turned_norms(upper_norms, lower_norms, coupling, cosine_last, sine_last)
    keep = skip != 0
    one, zero = jnp.ones_like(cosine), jnp.zeros_like(cosine)
    turns = (
        jnp.where(keep, one, cosine),
        jnp.where(keep, zero, sine),
        jnp.where(keep, one, cosine_last),
        jnp.where(keep, zero, sine_last),
    )
    return turns, jnp.where(keep, uu, upper_norms), jnp.where(keep, ll, right(lower_norms, second))


def turn(upper, lower, turns, first, second):
    gap = (second - first) & (BLOCK - 1)
    cosine, sine, cosine_last, sine_last = turns
    lower = left(lower, first)
    upper, lower = cosine * upper - sine * lower, sine * upper + cosine * lower
    lower = left(lower, gap)
    upper, lower = cosine_last * upper - sine_last * lower, sine_last * upper + cosine_last * lower
    return upper, right(lower, second)


def block_of(loads_ref, weights, block):
    columns = slice(block * BLOCK, (block + 1) * BLOCK)
    weight = weights[:, columns]
    return lambda start: loads_ref[start : start + GROUP, columns] * weight


def entries_kernel(offsets_ref, loads_ref, weights_ref, out_ref):
    rows = loads_ref.shape[0]
    weights = weights_ref[...]
    blocks = [block_of(loads_ref, weights, block) for block in range(4)]
    for pair in range(2):
        upper, lower = blocks[pair], blocks[2 + pair]
        out_ref[pair * PADDED : (pair + 1) * PADDED, :] = pair_entries(
            lambda start: (upper(start), lower(start)), rows, offsets_ref[0, 0], offsets_ref[0, 1]
        )


def first_turn_kernel(offsets_ref, skip_ref, place_ref, parts_ref, loads_ref, weights_ref,
                      even_ref, odd_ref, upper_ref, lower_ref):
    rows = loads_ref.shape[0]
    first, second = offsets_ref[0, 0], offsets_ref[0, 1]
    weights = weights_ref[...]
    blocks = [block_of(loads_ref, weights, block) for block in range(4)]
    total = parts_ref[0]
    for part in range(1, parts_ref.shape[0]):
        total = total + parts_ref[part]
    is_even = (place_ref[0] & 1) == 0
    turns = [
        pair_angles(total[pair * PADDED : (pair + 1) * PADDED], first, second, skip_ref[0, pair])[0]
        for pair in range(2)
    ]
    for start in range(0, rows, GROUP):
        span = slice(start, start + GROUP)
        upper_0, lower_0 = turn(blocks[0](start), blocks[2](start), turns[0], first, second)
        upper_1, lower_1 = turn(blocks[1](start), blocks[3](start), turns[1], first, second)
        upper_ref[span, :] = upper_0
        lower_ref[span, :] = lower_1
        even_ref[span, :] = jnp.where(is_even, upper_1, lower_0)
        odd_ref[span, :] = jnp.where(is_even, lower_0, upper_1)


def moved(place_ref, even_ref, odd_ref, upper_ref, lower_ref):
    is_even = (place_ref[0] & 1) == 0
    is_head = place_ref[0] == 0

    def load(start):
        span = slice(start, start + GROUP)
        even, odd, upper = even_ref[span, :], odd_ref[span, :], upper_ref[span, :]
        coming_upper = jnp.where(is_even, odd, even)
        coming_lower = jnp.where(is_even, even, odd)
        return (
            (jnp.where(is_head, upper, coming_upper), lower_ref[span, :]),
            (jnp.where(is_head, coming_upper, upper), coming_lower),
        )

    return load


def moved_entries_kernel(offsets_ref, place_ref, even_ref, odd_ref, upper_ref, lower_ref, out_ref):
    rows = even_ref.shape[0]
    load = moved(place_ref, even_ref, odd_ref, upper_ref, lower_ref)
    for pair in range(2):
        out_ref[pair * PADDED : (pair + 1) * PADDED, :] = pair_entries(
            lambda start: load(start)[pair], rows, offsets_ref[1, 0], offsets_ref[1, 1]
        )


def last_turn_kernel(total_rows, offsets_ref, skip_ref, place_ref, parts_ref, even_ref, odd_ref, upper_ref, lower_ref,
                     rotated_ref, power_ref):
    rows = even_ref.shape[0]
    first, second = offsets_ref[1, 0], offsets_ref[1, 1]
    load = moved(place_ref, even_ref, odd_ref, upper_ref, lower_ref)
    total = parts_ref[0]
    for part in range(1, parts_ref.shape[0]):
        total = total + parts_ref[part]
    turns = []
    for pair in range(2):
        own, upper_norms, lower_norms = pair_angles(
            total[pair * PADDED : (pair + 1) * PADDED], first, second, skip_ref[1, pair]
        )
        turns.append(own)
        power_ref[:, pair * BLOCK : (pair + 1) * BLOCK] = upper_norms / total_rows
        power_ref[:, (2 + pair) * BLOCK : (3 + pair) * BLOCK] = lower_norms / total_rows
    for start in range(0, rows, GROUP):
        span = slice(start, start + GROUP)
        for pair, (upper, lower) in enumerate(load(start)):
            upper, lower = turn(upper, lower, turns[pair], first, second)
            rotated_ref[span, pair * BLOCK : (pair + 1) * BLOCK] = upper
            rotated_ref[span, (2 + pair) * BLOCK : (3 + pair) * BLOCK] = lower


VMEM_LIMIT = 8 * 1024 * 1024
SMEM = pl.BlockSpec(memory_space=pltpu.SMEM)
VMEM = pl.BlockSpec(memory_space=pltpu.VMEM)


def call(kernel, scalars, arrays, shapes, name):
    several = isinstance(shapes, list)
    outs = [jax.ShapeDtypeStruct(shape, jnp.float32) for shape in (shapes if several else [shapes])]
    return pl.pallas_call(
        kernel,
        out_shape=outs if several else outs[0],
        in_specs=[SMEM] * len(scalars) + [VMEM] * len(arrays),
        out_specs=[VMEM] * len(outs) if several else VMEM,
        name=name,
        compiler_params=pltpu.CompilerParams(vmem_limit_bytes=VMEM_LIMIT),
    )(*scalars, *arrays)


def sum_parts(entries):
    size = lax.axis_size("rows")
    entries = entries + lax.ppermute(entries, "rows", [(row, row ^ 1) for row in range(size)])
    groups = [list(range(core, size, 2)) for core in range(2)]
    copies = jnp.broadcast_to(entries[None], (size // 2,) + entries.shape)
    return lax.all_to_all(copies, "rows", 0, 0, axis_index_groups=groups)


def per_device(loads, col_weights, partner_offsets, skip_mask):
    rows, columns = loads.shape
    pairs = lax.axis_size("pairs")
    place = lax.axis_index("pairs").reshape(1)
    weights = col_weights.reshape(1, columns)
    block = (rows, BLOCK)
    entries = call(entries_kernel, [partner_offsets], [loads, weights], (2 * PADDED, BLOCK), "entries")
    parts = sum_parts(entries)
    even, odd, upper, lower = call(
        first_turn_kernel, [partner_offsets, skip_mask, place], [parts, loads, weights], [block] * 4, "first_turn"
    )
    even = lax.ppermute(even, "pairs", [(at, at ^ 1) for at in range(pairs)])
    odd = lax.ppermute(odd, "pairs", [(at, min(max(((at + 1) ^ 1) - 1, 0), pairs - 1)) for at in range(pairs)])
    held = [even, odd, upper, lower]
    entries = call(moved_entries_kernel, [partner_offsets, place], held, (2 * PADDED, BLOCK), "moved_entries")
    parts = sum_parts(entries)
    total_rows = rows * lax.axis_size("rows")
    rotated, power = call(
        functools.partial(last_turn_kernel, float(total_rows)),
        [partner_offsets, skip_mask, place], [parts] + held, [(rows, columns), (1, columns)], "last_turn",
    )
    return rotated, power.reshape(columns)


def solution(mesh):
    in_specs = (P("rows", "pairs"), P("pairs"), P(), P(None, "pairs"))
    out_specs = (P("rows", "pairs"), P("pairs"))
    return jax.shard_map(
        per_device, mesh=mesh, in_specs=in_specs, out_specs=out_specs, check_vma=False
    )
```

```python
import functools
import jax
import jax.numpy as jnp
from jax import lax
from jax.experimental import pallas as pl
from jax.experimental.pallas import tpu as pltpu
from jax.sharding import PartitionSpec as P

BLOCK = 128
GROUP = 8
CHUNKS = 4

STATS = 19
CROSS = 2 * STATS
FLAGS = CROSS + 36
SUMS = 80
NORMS = 12
ANGLES = 16
VMEM_LIMIT = 8 * 1024 * 1024


def left(x, by):
    return pltpu.roll(x, (-by) & (BLOCK - 1), 1)


def right(x, by):
    return pltpu.roll(x, by & (BLOCK - 1), 1)


class Lags:
    def __init__(self, offsets, slot):
        place = lax.axis_index("pairs")
        self.first = offsets[0, 0]
        self.gap = offsets[0, 1] - offsets[0, 0]
        self.turn = offsets[1, 1] - offsets[1, 0]
        self.x_low = (slot == 1) & (place == 0)
        self.y_up = (slot == 1) & (place == lax.axis_size("pairs") - 1)
        self.x_shift = jnp.where(self.x_low, offsets[0, 1], 0)
        y_shift = jnp.where(self.y_up, 0, offsets[0, 1])
        self.lag = offsets[1, 0] - y_shift + self.x_shift
        self.out = self.x_shift + offsets[1, 1]

    def crossed(self):
        return (self.lag, self.lag + self.turn, self.lag - self.turn)


def halves(ref, span):
    return ref[span, :BLOCK], ref[span, BLOCK:]


def sums_over(rows, count, terms):
    def body(step, totals):
        span = pl.ds(pl.multiple_of(step * GROUP, GROUP), GROUP)
        return tuple(total + term for total, term in zip(totals, terms(span)))

    zeros = tuple(jnp.zeros((GROUP, BLOCK), jnp.float32) for _ in range(count))
    totals = lax.fori_loop(0, rows // GROUP, body, zeros, unroll=4)
    return [jnp.sum(total, axis=0, keepdims=True) for total in totals]


def store_rows(out_ref, start, values):
    for index, value in enumerate(values):
        out_ref[start + index : start + index + 1, :] = value


def lagged(x, y, lag, gap):
    terms = []
    for by in (lag - gap, lag, lag + gap):
        moved = [left(half, by) for half in y]
        terms += [a * b for a in x for b in moved]
    return terms


def pair_stats(ref, rows, lags):
    def terms(span):
        upper, lower = halves(ref, span)
        upper_gap, lower_gap = left(upper, lags.gap), left(lower, lags.gap)
        step_0 = [upper * upper, lower * lower, upper * lower, upper * lower_gap, upper_gap * lower, upper * upper_gap, lower * lower_gap]
        return step_0 + lagged((upper, lower), (upper, lower), lags.turn, lags.gap)

    return sums_over(rows, STATS, terms)


def angle(first_norms, second_norms, coupling):
    half_gap = 0.5 * (second_norms - first_norms)
    gap_sign = jnp.where(half_gap >= 0.0, 1.0, -1.0)
    denominator = jnp.maximum(
        jnp.abs(half_gap) + jnp.sqrt(half_gap * half_gap + coupling * coupling),
        1e-06 * (first_norms + second_norms),
    )
    tangent = gap_sign * coupling / denominator
    cosine = 1.0 / jnp.sqrt(1.0 + tangent * tangent)
    return cosine, tangent * cosine


def turned_norms(first_norms, second_norms, coupling, cosine, sine):
    new_first = cosine * (cosine * first_norms - sine * coupling) - sine * (cosine * coupling - sine * second_norms)
    new_second = sine * (sine * first_norms + cosine * coupling) + cosine * (sine * coupling + cosine * second_norms)
    return new_first, new_second


def two_rounds(first_norms, second_norms, couplings, gap, keep):
    same, ahead, behind, firsts, seconds = couplings
    cosine, sine = angle(first_norms, second_norms, same)
    new_first, new_second = turned_norms(first_norms, second_norms, same, cosine, sine)
    cosine_gap, sine_gap = left(cosine, gap), left(sine, gap)
    coupling = cosine * (sine_gap * firsts + cosine_gap * ahead) - sine * (sine_gap * behind + cosine_gap * seconds)
    new_second = left(new_second, gap)
    cosine_last, sine_last = angle(new_first, new_second, coupling)
    new_first, new_second = turned_norms(new_first, new_second, coupling, cosine_last, sine_last)
    one, zero = jnp.ones_like(cosine), jnp.zeros_like(cosine)
    turns = (
        jnp.where(keep, one, cosine),
        jnp.where(keep, zero, sine),
        jnp.where(keep, one, cosine_last),
        jnp.where(keep, zero, sine_last),
    )
    return turns, (jnp.where(keep, first_norms, new_first), jnp.where(keep, left(second_norms, gap), new_second))


def joint(x_weights, y_weights, dots, gap):
    total = None
    for a in range(2):
        for b in range(2):
            (x_here, x_gap), (y_here, y_gap) = x_weights[a], y_weights[b]
            before, at, after = [dots[4 * index + 2 * a + b] for index in range(3)]
            part = x_here * (y_here * at + y_gap * after) + x_gap * (y_here * left(before, gap) + y_gap * left(at, gap))
            total = part if total is None else total + part
    return total


def rolled(weights, by):
    return [[left(value, by) for value in pair] for pair in weights]


def load_kernel(offsets_hbm, skip_hbm, loads_hbm, weights_hbm, first_ref, second_ref, offsets, skip, loads, weights, sems):
    rows = loads.shape[0]
    part = rows // CHUNKS
    small = [
        pltpu.make_async_copy(offsets_hbm, offsets, sems.at[CHUNKS]),
        pltpu.make_async_copy(skip_hbm, skip, sems.at[CHUNKS + 1]),
        pltpu.make_async_copy(weights_hbm, weights, sems.at[CHUNKS + 2]),
    ]
    large = [
        pltpu.make_async_copy(loads_hbm.at[pl.ds(chunk * part, part)], loads.at[pl.ds(chunk * part, part)], sems.at[chunk])
        for chunk in range(CHUNKS)
    ]
    for copy in small + large:
        copy.start()
    for copy in small:
        copy.wait()
    is_even = (lax.axis_index("pairs") & 1) == 0
    first = offsets[0, 0]
    weight = [weights[:, block * BLOCK : (block + 1) * BLOCK] for block in range(4)]
    for chunk in range(CHUNKS):
        large[chunk].wait()

        def body(step, _):
            span = pl.ds(pl.multiple_of(chunk * part + step * GROUP, GROUP), GROUP)
            blocks = [loads[span, block * BLOCK : (block + 1) * BLOCK] * weight[block] for block in range(4)]
            lower_0, lower_1 = left(blocks[2], first), left(blocks[3], first)
            first_ref[span, :BLOCK] = jnp.where(is_even, blocks[1], blocks[0])
            first_ref[span, BLOCK:] = jnp.where(is_even, lower_1, lower_0)
            second_ref[span, :BLOCK] = jnp.where(is_even, blocks[0], blocks[1])
            second_ref[span, BLOCK:] = jnp.where(is_even, lower_0, lower_1)
            return _

        lax.fori_loop(0, part // GROUP, body, 0, unroll=4)
    span = slice(rows, rows + GROUP)
    skips = [skip[0, pair].astype(jnp.float32) for pair in range(2)]
    first_ref[span, :] = jnp.full((GROUP, 2 * BLOCK), jnp.where(is_even, skips[1], skips[0]), jnp.float32)
    second_ref[span, :] = jnp.full((GROUP, 2 * BLOCK), jnp.where(is_even, skips[0], skips[1]), jnp.float32)


def stats_kernel(rows, offsets, first_ref, second_ref, first_out, second_out):
    lags = Lags(offsets, 0)
    for ref, out in ((first_ref, first_out), (second_ref, second_out)):
        store_rows(out, 0, pair_stats(ref, rows, lags))


def cross_kernel(rows, odd_slot, offsets, skip, own_ref, come_ref, stats_ref, out_ref):
    is_even = (lax.axis_index("pairs") & 1) == 0
    slot = jnp.where(is_even, 1 - odd_slot, odd_slot)
    lags = Lags(offsets, slot)
    own_first = slot == 1
    come_stats = pair_stats(come_ref, rows, lags)
    own_flag, come_flag = [ref[rows : rows + 1, :BLOCK] for ref in (own_ref, come_ref)]
    step_flag = jnp.full((1, BLOCK), jnp.where(own_first, skip[1, 1], skip[1, 0]).astype(jnp.float32), jnp.float32)
    own_stats = [stats_ref[index : index + 1, :] for index in range(STATS)]

    def fill(x_ref, y_ref, x_stats, y_stats, flags):
        store_rows(out_ref, 0, x_stats)
        store_rows(out_ref, STATS, y_stats)
        for index, lag in enumerate(lags.crossed()):
            sums = sums_over(rows, 12, lambda span: lagged(halves(x_ref, span), halves(y_ref, span), lag, lags.gap))
            store_rows(out_ref, CROSS + 12 * index, sums)
        store_rows(out_ref, FLAGS, flags + [jnp.zeros((1, BLOCK), jnp.float32)] * (SUMS - FLAGS - 3))

    @pl.when(own_first)
    def _():
        fill(own_ref, come_ref, own_stats, come_stats, [own_flag, come_flag, step_flag])

    @pl.when(jnp.logical_not(own_first))
    def _():
        fill(come_ref, own_ref, come_stats, own_stats, [come_flag, own_flag, step_flag])


def angles_kernel(total_rows, offsets, sums_ref, out_ref):
    lags = Lags(offsets, lax.axis_index("rows") & 1)
    rows = [sums_ref[index : index + 1, :] for index in range(FLAGS + 3)]
    sides = []
    for side, is_low in ((0, lags.x_low), (1, jnp.logical_not(lags.y_up))):
        stats = rows[side * STATS : (side + 1) * STATS]
        (cosine, sine, cosine_last, sine_last), norms = two_rounds(stats[0], stats[1], stats[2:7], lags.gap, rows[FLAGS + side] > 0.5)
        here = jnp.where(is_low, sine_last, cosine_last)
        ahead = jnp.where(is_low, cosine_last, -sine_last)
        weights = [
            [here * cosine, ahead * left(sine, lags.gap)],
            [-here * sine, ahead * left(cosine, lags.gap)],
        ]
        sides.append((jnp.where(is_low, norms[1], norms[0]), weights, stats[7:], [cosine, sine, here, ahead]))
    (x_norms, x_weights, x_dots, x_turns), (y_norms, y_weights, y_dots, y_turns) = sides
    crossed = [
        joint(x_weights, rolled(y_weights, lag), rows[CROSS + 12 * index : CROSS + 12 * (index + 1)], lags.gap)
        for index, lag in enumerate(lags.crossed())
    ]
    firsts = joint(x_weights, rolled(x_weights, lags.turn), x_dots, lags.gap)
    seconds = left(joint(y_weights, rolled(y_weights, lags.turn), y_dots, lags.gap), lags.lag)
    couplings = (crossed[0], crossed[1], left(crossed[2], lags.turn), firsts, seconds)
    turns, (upper, lower) = two_rounds(x_norms, left(y_norms, lags.lag), couplings, lags.turn, rows[FLAGS + 2] > 0.5)
    norms = [right(upper, lags.x_shift) / total_rows, right(lower, lags.out) / total_rows]
    store_rows(out_ref, 0, x_turns + y_turns + list(turns) + norms + [jnp.zeros_like(upper)] * (ANGLES - NORMS - 2))


def last_kernel(offsets, mine_ref, other_ref, first_ref, second_ref, first_come, second_come,
                rotated_hbm, power_ref, rotated, sems):
    rows = rotated.shape[0]
    part = rows // CHUNKS
    is_even = (lax.axis_index("pairs") & 1) == 0
    on_first_core = (lax.axis_index("rows") & 1) == 0
    mine, other = mine_ref[...], other_ref[...]
    angles = [jnp.where(on_first_core, mine, other), jnp.where(on_first_core, other, mine)]
    lags = [Lags(offsets, slot) for slot in range(2)]
    for slot in range(2):
        power_ref[:, slot * BLOCK : (slot + 1) * BLOCK] = angles[slot][NORMS : NORMS + 1]
        power_ref[:, (2 + slot) * BLOCK : (3 + slot) * BLOCK] = angles[slot][NORMS + 1 : NORMS + 2]

    def turn(x, y, cosine, sine):
        return cosine * x - sine * y, sine * x + cosine * y

    def block_after(ref, span, values, gap):
        cosine, sine, here, ahead = values
        upper, lower = turn(*halves(ref, span), cosine, sine)
        return here * upper + ahead * left(lower, gap)

    def fill(sources):
        copies = []
        for chunk in range(CHUNKS):

            def body(step, _):
                span = pl.ds(pl.multiple_of(chunk * part + step * GROUP, GROUP), GROUP)
                for slot, (x_ref, y_ref) in enumerate(sources):
                    lag, values = lags[slot], [angles[slot][index : index + 1] for index in range(NORMS)]
                    upper = block_after(x_ref, span, values[:4], lag.gap)
                    lower = left(block_after(y_ref, span, values[4:8], lag.gap), lag.lag)
                    upper, lower = turn(upper, lower, values[8], values[9])
                    upper, lower = turn(upper, left(lower, lag.turn), values[10], values[11])
                    rotated[span, slot * BLOCK : (slot + 1) * BLOCK] = right(upper, lag.x_shift) if slot else upper
                    rotated[span, (2 + slot) * BLOCK : (3 + slot) * BLOCK] = right(lower, lag.out)
                return _

            lax.fori_loop(0, part // GROUP, body, 0, unroll=2)
            place = pl.ds(chunk * part, part)
            copy = pltpu.make_async_copy(rotated.at[place], rotated_hbm.at[place], sems.at[chunk])
            copy.start()
            copies.append(copy)
        for copy in copies:
            copy.wait()

    @pl.when(is_even)
    def _():
        fill([(second_come, first_ref), (second_ref, first_come)])

    @pl.when(jnp.logical_not(is_even))
    def _():
        fill([(first_come, second_ref), (first_ref, second_come)])


SMEM = pl.BlockSpec(memory_space=pltpu.SMEM)
VMEM = pl.BlockSpec(memory_space=pltpu.VMEM)
HBM = pl.BlockSpec(memory_space=pltpu.HBM)


def call(kernel, operands, outs, name, scratch=(), micros=1):
    return pl.pallas_call(
        kernel,
        out_shape=[jax.ShapeDtypeStruct(shape, jnp.float32) for shape, _ in outs],
        in_specs=[space for _, space in operands],
        out_specs=[space for _, space in outs],
        scratch_shapes=scratch,
        name=name,
        cost_estimate=pl.CostEstimate(flops=micros * 10**9, bytes_accessed=micros * 10**6, transcendentals=0),
        compiler_params=pltpu.CompilerParams(vmem_limit_bytes=VMEM_LIMIT),
    )(*[array for array, _ in operands])


def swap_rows(x, partner):
    size = lax.axis_size("rows")
    depth = size // 4

    def other(row):
        y, z, core = partner(row // (2 * depth), (row // 2) % depth, row % 2)
        return (y * depth + z) * 2 + core

    return lax.ppermute(x, "rows", [(row, other(row)) for row in range(size)])


OPPOSITE = (6, 7, 4, 5, 2, 3, 0, 1)


def per_device(loads, col_weights, partner_offsets, skip_mask):
    rows, columns = loads.shape
    pairs = lax.axis_size("pairs")
    weights = col_weights.reshape(1, columns)
    held = (rows + GROUP, 2 * BLOCK)
    first, second = call(
        load_kernel,
        [(partner_offsets, HBM), (skip_mask, HBM), (loads, HBM), (weights, HBM)],
        [(held, VMEM)] * 2,
        "load",
        [
            pltpu.SMEM(partner_offsets.shape, jnp.int32),
            pltpu.SMEM(skip_mask.shape, jnp.int32),
            pltpu.VMEM((rows, columns), jnp.float32),
            pltpu.VMEM((1, columns), jnp.float32),
            pltpu.SemaphoreType.DMA((CHUNKS + 3,)),
        ],
    )
    first_come = lax.ppermute(first, "pairs", [(at, at ^ 1) for at in range(pairs)])
    second_come = lax.ppermute(second, "pairs", [(at, min(max(((at + 1) ^ 1) - 1, 0), pairs - 1)) for at in range(pairs)])
    offsets, skips = (partner_offsets, SMEM), (skip_mask, SMEM)
    first_stats, second_stats = call(
        functools.partial(stats_kernel, rows), [offsets, (first, VMEM), (second, VMEM)], [((24, BLOCK), VMEM)] * 2, "stats"
    )
    slots = []
    for odd_slot, own, come, stats in ((0, second, first_come, second_stats), (1, first, second_come, first_stats)):
        slots += call(
            functools.partial(cross_kernel, rows, odd_slot),
            [offsets, skips, (own, VMEM), (come, VMEM), (stats, VMEM)],
            [((SUMS, BLOCK), VMEM)],
            "cross",
        )
    keeps_first = (lax.axis_index("pairs") & 1) == (lax.axis_index("rows") & 1)
    sums = jnp.where(keeps_first, slots[1], slots[0])
    sums = sums + swap_rows(jnp.where(keeps_first, slots[0], slots[1]), lambda y, z, core: (y, z, 1 - core))
    sums = sums + swap_rows(sums, lambda y, z, core: (1 - y, z, core))
    sums = sums + swap_rows(sums, lambda y, z, core: (y, z ^ 1, core))
    sums = sums + swap_rows(sums, lambda y, z, core: (y, z ^ 2, core))
    sums = sums + swap_rows(sums, lambda y, z, core: (y, OPPOSITE[z], core))
    total_rows = float(rows * lax.axis_size("rows"))
    (angles,) = call(functools.partial(angles_kernel, total_rows), [offsets, (sums, VMEM)], [((ANGLES, BLOCK), VMEM)], "angles")
    other = swap_rows(angles, lambda y, z, core: (y, z, 1 - core))
    rotated, power = call(
        last_kernel,
        [offsets] + [(array, VMEM) for array in (angles, other, first, second, first_come, second_come)],
        [((rows, columns), HBM), ((1, columns), VMEM)],
        "last",
        [pltpu.VMEM((rows, columns), jnp.float32), pltpu.SemaphoreType.DMA((CHUNKS,))],
    )
    return rotated, power.reshape(columns)


def solution(mesh):
    in_specs = (P("rows", "pairs"), P("pairs"), P(), P(None, "pairs"))
    out_specs = (P("rows", "pairs"), P("pairs"))
    return jax.shard_map(
        per_device, mesh=mesh, in_specs=in_specs, out_specs=out_specs, check_vma=False
    )
```

```python
import functools
import jax
import jax.numpy as jnp
from jax import lax
from jax.experimental import pallas as pl
from jax.experimental.pallas import tpu as pltpu
from jax.sharding import PartitionSpec as P

BLOCK = 128
GROUP = 8
BATCH = 128

STATS = 19
CROSS = 2 * STATS
FLAGS = CROSS + 36
SUMS = 80
NORMS = 12
ANGLES = 16
VMEM_LIMIT = 8 * 1024 * 1024


def left(x, by):
    return pltpu.roll(x, (-by) & (BLOCK - 1), 1)


def right(x, by):
    return pltpu.roll(x, by & (BLOCK - 1), 1)


class Lags:
    def __init__(self, offsets, slot):
        place = lax.axis_index("pairs")
        self.first = offsets[0, 0]
        self.gap = offsets[0, 1] - offsets[0, 0]
        self.turn = offsets[1, 1] - offsets[1, 0]
        self.x_low = (slot == 1) & (place == 0)
        self.y_up = (slot == 1) & (place == lax.axis_size("pairs") - 1)
        self.x_shift = jnp.where(self.x_low, offsets[0, 1], 0)
        y_shift = jnp.where(self.y_up, 0, offsets[0, 1])
        self.lag = offsets[1, 0] - y_shift + self.x_shift
        self.out = self.x_shift + offsets[1, 1]

    def crossed(self):
        return (self.lag, self.lag + self.turn, self.lag - self.turn)


def halves(ref, span):
    return ref[span, :BLOCK], ref[span, BLOCK:]


def sums_over(rows, terms):
    totals = None
    for start in range(0, rows, BATCH):
        parts = [jnp.sum(term.reshape(BATCH // GROUP, GROUP, BLOCK), axis=0) for term in terms(slice(start, start + BATCH))]
        totals = parts if totals is None else [total + part for total, part in zip(totals, parts)]
    return [jnp.sum(total, axis=0, keepdims=True) for total in totals]


def store_rows(out_ref, start, values):
    for index, value in enumerate(values):
        out_ref[start + index : start + index + 1, :] = value


def lagged(x, y, lag, gap):
    terms = []
    for by in (lag - gap, lag, lag + gap):
        moved = [left(half, by) for half in y]
        terms += [a * b for a in x for b in moved]
    return terms


def pair_stats(ref, rows, lags):
    def terms(span):
        upper, lower = halves(ref, span)
        upper_gap, lower_gap = left(upper, lags.gap), left(lower, lags.gap)
        step_0 = [upper * upper, lower * lower, upper * lower, upper * lower_gap, upper_gap * lower, upper * upper_gap, lower * lower_gap]
        return step_0 + lagged((upper, lower), (upper, lower), lags.turn, lags.gap)

    return sums_over(rows, terms)


def angle(first_norms, second_norms, coupling):
    half_gap = 0.5 * (second_norms - first_norms)
    gap_sign = jnp.where(half_gap >= 0.0, 1.0, -1.0)
    denominator = jnp.maximum(
        jnp.abs(half_gap) + jnp.sqrt(half_gap * half_gap + coupling * coupling),
        1e-06 * (first_norms + second_norms),
    )
    tangent = gap_sign * coupling / denominator
    cosine = 1.0 / jnp.sqrt(1.0 + tangent * tangent)
    return cosine, tangent * cosine


def turned_norms(first_norms, second_norms, coupling, cosine, sine):
    new_first = cosine * (cosine * first_norms - sine * coupling) - sine * (cosine * coupling - sine * second_norms)
    new_second = sine * (sine * first_norms + cosine * coupling) + cosine * (sine * coupling + cosine * second_norms)
    return new_first, new_second


def two_rounds(first_norms, second_norms, couplings, gap, keep):
    same, ahead, behind, firsts, seconds = couplings
    cosine, sine = angle(first_norms, second_norms, same)
    new_first, new_second = turned_norms(first_norms, second_norms, same, cosine, sine)
    cosine_gap, sine_gap = left(cosine, gap), left(sine, gap)
    coupling = cosine * (sine_gap * firsts + cosine_gap * ahead) - sine * (sine_gap * behind + cosine_gap * seconds)
    new_second = left(new_second, gap)
    cosine_last, sine_last = angle(new_first, new_second, coupling)
    new_first, new_second = turned_norms(new_first, new_second, coupling, cosine_last, sine_last)
    one, zero = jnp.ones_like(cosine), jnp.zeros_like(cosine)
    turns = (
        jnp.where(keep, one, cosine),
        jnp.where(keep, zero, sine),
        jnp.where(keep, one, cosine_last),
        jnp.where(keep, zero, sine_last),
    )
    return turns, (jnp.where(keep, first_norms, new_first), jnp.where(keep, left(second_norms, gap), new_second))


def joint(x_weights, y_weights, dots, gap):
    total = None
    for a in range(2):
        for b in range(2):
            (x_here, x_gap), (y_here, y_gap) = x_weights[a], y_weights[b]
            before, at, after = [dots[4 * index + 2 * a + b] for index in range(3)]
            part = x_here * (y_here * at + y_gap * after) + x_gap * (y_here * left(before, gap) + y_gap * left(at, gap))
            total = part if total is None else total + part
    return total


def rolled(weights, by):
    return [[left(value, by) for value in pair] for pair in weights]


def load_kernel(offsets_hbm, skip_hbm, loads_hbm, weights_hbm, first_hbm, second_hbm,
                offsets, skip, loads, weights, held, in_sems, out_sems):
    rows = loads.shape[0]
    parts = range(0, rows, BATCH)
    small = [(offsets_hbm, offsets), (skip_hbm, skip), (weights_hbm, weights)]
    large = [(loads_hbm.at[pl.ds(start, BATCH)], loads.at[pl.ds(start, BATCH)]) for start in parts]
    copies = [pltpu.make_async_copy(*ends, in_sems.at[at]) for at, ends in enumerate(small + large)]
    for copy in copies:
        copy.start()
    for copy in copies[:3]:
        copy.wait()
    is_even = (lax.axis_index("pairs") & 1) == 0
    skips = [skip[0, pair].astype(jnp.float32) for pair in range(2)]
    for at, order in enumerate((skips[::-1], skips)):
        held[at, rows:, :] = jnp.full((GROUP, 2 * BLOCK), jnp.where(is_even, *order), jnp.float32)
    weight = [weights[:, block * BLOCK : (block + 1) * BLOCK] for block in range(4)]
    sent = []
    for part, start in enumerate(parts):
        copies[3 + part].wait()
        span = slice(start, start + BATCH)
        blocks = [loads[span, block * BLOCK : (block + 1) * BLOCK] * weight[block] for block in range(4)]
        blocks = blocks[:2] + [left(block, offsets[0, 0]) for block in blocks[2:]]
        last = start + BATCH == rows
        for at, out in enumerate((first_hbm, second_hbm)):
            for half in range(2):
                even, odd = blocks[2 * half + 1 - at], blocks[2 * half + at]
                held[at, span, half * BLOCK : (half + 1) * BLOCK] = jnp.where(is_even, even, odd)
            place = pl.ds(start, BATCH + GROUP if last else BATCH)
            sent.append(pltpu.make_async_copy(held.at[at, place], out.at[place], out_sems.at[at, part]))
            sent[-1].start()
    for copy in sent:
        copy.wait()


def stats_kernel(rows, offsets, first_ref, second_ref, first_out, second_out):
    lags = Lags(offsets, 0)
    for ref, out in ((first_ref, first_out), (second_ref, second_out)):
        store_rows(out, 0, pair_stats(ref, rows, lags))


def cross_kernel(rows, odd_slot, offsets, skip, own_ref, come_ref, stats_ref, out_ref):
    is_even = (lax.axis_index("pairs") & 1) == 0
    slot = jnp.where(is_even, 1 - odd_slot, odd_slot)
    lags = Lags(offsets, slot)
    own_first = slot == 1
    come_stats = pair_stats(come_ref, rows, lags)
    own_flag, come_flag = [ref[rows : rows + 1, :BLOCK] for ref in (own_ref, come_ref)]
    step_flag = jnp.full((1, BLOCK), jnp.where(own_first, skip[1, 1], skip[1, 0]).astype(jnp.float32), jnp.float32)
    own_stats = [stats_ref[index : index + 1, :] for index in range(STATS)]

    def pick(mine, theirs):
        return [jnp.where(own_first, a, b) for a, b in zip(mine, theirs)], [jnp.where(own_first, b, a) for a, b in zip(mine, theirs)]

    for start, stats in zip((0, STATS), pick(own_stats, come_stats)):
        store_rows(out_ref, start, stats)
    for index, lag in enumerate(lags.crossed()):
        sums = sums_over(rows, lambda span: lagged(*pick(halves(own_ref, span), halves(come_ref, span)), lag, lags.gap))
        store_rows(out_ref, CROSS + 12 * index, sums)
    x_flag, y_flag = pick([own_flag], [come_flag])
    store_rows(out_ref, FLAGS, x_flag + y_flag + [step_flag] + [jnp.zeros((1, BLOCK), jnp.float32)] * (SUMS - FLAGS - 3))


def angles_kernel(total_rows, offsets, sums_ref, out_ref):
    lags = Lags(offsets, lax.axis_index("rows") & 1)
    rows = [sums_ref[index : index + 1, :] for index in range(FLAGS + 3)]
    sides = []
    for side, is_low in ((0, lags.x_low), (1, jnp.logical_not(lags.y_up))):
        stats = rows[side * STATS : (side + 1) * STATS]
        (cosine, sine, cosine_last, sine_last), norms = two_rounds(stats[0], stats[1], stats[2:7], lags.gap, rows[FLAGS + side] > 0.5)
        here = jnp.where(is_low, sine_last, cosine_last)
        ahead = jnp.where(is_low, cosine_last, -sine_last)
        weights = [
            [here * cosine, ahead * left(sine, lags.gap)],
            [-here * sine, ahead * left(cosine, lags.gap)],
        ]
        sides.append((jnp.where(is_low, norms[1], norms[0]), weights, stats[7:], [cosine, sine, here, ahead]))
    (x_norms, x_weights, x_dots, x_turns), (y_norms, y_weights, y_dots, y_turns) = sides
    crossed = [
        joint(x_weights, rolled(y_weights, lag), rows[CROSS + 12 * index : CROSS + 12 * (index + 1)], lags.gap)
        for index, lag in enumerate(lags.crossed())
    ]
    firsts = joint(x_weights, rolled(x_weights, lags.turn), x_dots, lags.gap)
    seconds = left(joint(y_weights, rolled(y_weights, lags.turn), y_dots, lags.gap), lags.lag)
    couplings = (crossed[0], crossed[1], left(crossed[2], lags.turn), firsts, seconds)
    turns, (upper, lower) = two_rounds(x_norms, left(y_norms, lags.lag), couplings, lags.turn, rows[FLAGS + 2] > 0.5)
    norms = [right(upper, lags.x_shift) / total_rows, right(lower, lags.out) / total_rows]
    store_rows(out_ref, 0, x_turns + y_turns + list(turns) + norms + [jnp.zeros_like(upper)] * (ANGLES - NORMS - 2))


def turn(x, y, cosine, sine):
    return cosine * x - sine * y, sine * x + cosine * y


def block_after(pair, turns, gap):
    cosine, sine, here, ahead = turns
    upper, lower = turn(*pair, cosine, sine)
    return here * upper + ahead * left(lower, gap)


def last_kernel(offsets, mine_ref, other_ref, first_ref, second_ref, first_come, second_come,
                rotated_hbm, power_hbm, rotated, power, sems):
    rows = rotated.shape[0]
    is_even = (lax.axis_index("pairs") & 1) == 0
    on_first_core = (lax.axis_index("rows") & 1) == 0
    mine, other = mine_ref[...], other_ref[...]
    sources = (((second_come, first_come), (first_ref, second_ref)), ((second_ref, first_ref), (first_come, second_come)))
    slots = [jnp.where(on_first_core, mine, other), jnp.where(on_first_core, other, mine)]
    for slot in range(2):
        for half in range(2):
            at = 2 * half + slot
            power[:, at * BLOCK : (at + 1) * BLOCK] = slots[slot][NORMS + half : NORMS + half + 1]
    copies = [pltpu.make_async_copy(power, power_hbm, sems.at[4])]
    copies[0].start()
    for slot, angles in enumerate(slots):
        lags = Lags(offsets, slot)
        blocks = [slice(at * BLOCK, (at + 1) * BLOCK) for at in (slot, 2 + slot)]
        turns = [angles[index : index + 1] for index in range(NORMS)]
        for start in range(0, rows, BATCH):
            span = slice(start, start + BATCH)
            x, y = [
                [jnp.where(is_even, a, b) for a, b in zip(halves(even_ref, span), halves(odd_ref, span))]
                for even_ref, odd_ref in sources[slot]
            ]
            upper = block_after(x, turns[:4], lags.gap)
            lower = left(block_after(y, turns[4:8], lags.gap), lags.lag)
            upper, lower = turn(upper, lower, turns[8], turns[9])
            upper, lower = turn(upper, left(lower, lags.turn), turns[10], turns[11])
            rotated[span, blocks[0]] = right(upper, lags.x_shift) if slot else upper
            rotated[span, blocks[1]] = right(lower, lags.out)
        for half, columns in enumerate(blocks):
            copies.append(pltpu.make_async_copy(rotated.at[:, columns], rotated_hbm.at[:, columns], sems.at[2 * slot + half]))
            copies[-1].start()
    for copy in copies:
        copy.wait()


VMEM = pl.BlockSpec(memory_space=pltpu.VMEM)
HBM = pl.BlockSpec(memory_space=pltpu.HBM)


def call(kernel, operands, outs, name, scratch=(), micros=1, grant=VMEM_LIMIT):
    return pl.pallas_call(
        kernel,
        out_shape=[jax.ShapeDtypeStruct(shape, jnp.float32) for shape, _ in outs],
        in_specs=[space for _, space in operands],
        out_specs=[space for _, space in outs],
        scratch_shapes=scratch,
        name=name,
        cost_estimate=pl.CostEstimate(flops=micros * 10**9, bytes_accessed=micros * 10**6, transcendentals=0),
        compiler_params=pltpu.CompilerParams(vmem_limit_bytes=grant),
    )(*[array for array, _ in operands])


def swap_rows(x, partner):
    size = lax.axis_size("rows")
    depth = size // 4

    def other(row):
        y, z, core = partner(row // (2 * depth), (row // 2) % depth, row % 2)
        return (y * depth + z) * 2 + core

    return lax.ppermute(x, "rows", [(row, other(row)) for row in range(size)])


OPPOSITE = (6, 7, 4, 5, 2, 3, 0, 1)


def per_device(loads, col_weights, partner_offsets, skip_mask):
    rows, columns = loads.shape
    pairs = lax.axis_size("pairs")
    weights = col_weights.reshape(1, columns)
    held = (rows + GROUP, 2 * BLOCK)
    first, second = call(
        load_kernel,
        [(partner_offsets, HBM), (skip_mask, HBM), (loads, HBM), (weights, HBM)],
        [(held, HBM)] * 2,
        "load",
        [
            pltpu.VMEM(partner_offsets.shape, jnp.int32),
            pltpu.VMEM(skip_mask.shape, jnp.int32),
            pltpu.VMEM((rows, columns), jnp.float32),
            pltpu.VMEM((1, columns), jnp.float32),
            pltpu.VMEM((2,) + held, jnp.float32),
            pltpu.SemaphoreType.DMA((3 + rows // BATCH,)),
            pltpu.SemaphoreType.DMA((2, rows // BATCH)),
        ],
        grant=None,
    )
    first_come = lax.ppermute(first, "pairs", [(at, at ^ 1) for at in range(pairs)])
    second_come = lax.ppermute(second, "pairs", [(at, min(max(((at + 1) ^ 1) - 1, 0), pairs - 1)) for at in range(pairs)])
    offsets, skips = (partner_offsets, VMEM), (skip_mask, VMEM)
    first_stats, second_stats = call(
        functools.partial(stats_kernel, rows), [offsets, (first, VMEM), (second, VMEM)], [((24, BLOCK), VMEM)] * 2, "stats"
    )
    slots = []
    for odd_slot, own, come, stats in ((0, second, first_come, second_stats), (1, first, second_come, first_stats)):
        slots += call(
            functools.partial(cross_kernel, rows, odd_slot),
            [offsets, skips, (own, VMEM), (come, VMEM), (stats, VMEM)],
            [((SUMS, BLOCK), VMEM)],
            "cross",
        )
    keeps_first = (lax.axis_index("pairs") & 1) == (lax.axis_index("rows") & 1)
    sums = jnp.where(keeps_first, slots[1], slots[0])
    sums = sums + swap_rows(jnp.where(keeps_first, slots[0], slots[1]), lambda y, z, core: (y, z, 1 - core))
    sums = sums + swap_rows(sums, lambda y, z, core: (1 - y, z, core))
    sums = sums + swap_rows(sums, lambda y, z, core: (y, z ^ 1, core))
    sums = sums + swap_rows(sums, lambda y, z, core: (y, z ^ 2, core))
    sums = sums + swap_rows(sums, lambda y, z, core: (y, OPPOSITE[z], core))
    total_rows = float(rows * lax.axis_size("rows"))
    (angles,) = call(functools.partial(angles_kernel, total_rows), [offsets, (sums, VMEM)], [((ANGLES, BLOCK), VMEM)], "angles")
    other = swap_rows(angles, lambda y, z, core: (y, z, 1 - core))
    rotated, power = call(
        last_kernel,
        [offsets] + [(array, VMEM) for array in (angles, other, first, second, first_come, second_come)],
        [((rows, columns), HBM), ((1, columns), HBM)],
        "last",
        [pltpu.VMEM((rows, columns), jnp.float32), pltpu.VMEM((1, columns), jnp.float32), pltpu.SemaphoreType.DMA((5,))],
    )
    return rotated, power.reshape(columns)


def solution(mesh):
    in_specs = (P("rows", "pairs"), P("pairs"), P(), P(None, "pairs"))
    out_specs = (P("rows", "pairs"), P("pairs"))
    return jax.shard_map(
        per_device, mesh=mesh, in_specs=in_specs, out_specs=out_specs, check_vma=False
    )
```

```python
import functools
import jax
import jax.numpy as jnp
from jax import lax
from jax.experimental import pallas as pl
from jax.experimental.pallas import tpu as pltpu
from jax.sharding import PartitionSpec as P

BLOCK = 128
GROUP = 8
BATCH = 128

STATS = 19
CROSS = 2 * STATS
FLAGS = CROSS + 36
SUMS = 80
NORMS = 12
ANGLES = 16
VMEM_LIMIT = 8 * 1024 * 1024


def left(x, by):
    return pltpu.roll(x, (-by) & (BLOCK - 1), 1)


def right(x, by):
    return pltpu.roll(x, by & (BLOCK - 1), 1)


def at_end():
    place = lax.axis_index("pairs")
    return (place == 0) | (place == lax.axis_size("pairs") - 1)


class Lags:
    def __init__(self, offsets, slot):
        place = lax.axis_index("pairs")
        self.first = offsets[0, 0]
        self.gap = offsets[0, 1] - offsets[0, 0]
        self.turn = offsets[1, 1] - offsets[1, 0]
        self.x_low = (slot == 1) & (place == 0)
        self.y_up = (slot == 1) & (place == lax.axis_size("pairs") - 1)
        self.x_shift = jnp.where(self.x_low, offsets[0, 1], 0)
        y_shift = jnp.where(self.y_up, 0, offsets[0, 1])
        self.lag = offsets[1, 0] - y_shift + self.x_shift
        self.out = self.x_shift + offsets[1, 1]

    def crossed(self):
        return (self.lag, self.lag + self.turn, self.lag - self.turn)


def halves(ref, span):
    return ref[span, :BLOCK], ref[span, BLOCK:]


def sums_over(rows, terms):
    totals = None
    for start in range(0, rows, BATCH):
        parts = [jnp.sum(term.reshape(BATCH // GROUP, GROUP, BLOCK), axis=0) for term in terms(slice(start, start + BATCH))]
        totals = parts if totals is None else [total + part for total, part in zip(totals, parts)]
    return [jnp.sum(total, axis=0, keepdims=True) for total in totals]


def store_rows(out_ref, start, values):
    for index, value in enumerate(values):
        out_ref[start + index : start + index + 1, :] = value


def lagged(x, y, lag, gap):
    terms = []
    for by in (lag - gap, lag, lag + gap):
        moved = [left(half, by) for half in y]
        terms += [a * b for a in x for b in moved]
    return terms


def pair_stats(pair_at, rows, lags):
    def terms(span):
        upper, lower = pair_at(span)
        upper_gap, lower_gap = left(upper, lags.gap), left(lower, lags.gap)
        step_0 = [upper * upper, lower * lower, upper * lower, upper * lower_gap, upper_gap * lower, upper * upper_gap, lower * lower_gap]
        return step_0 + lagged((upper, lower), (upper, lower), lags.turn, lags.gap)

    return sums_over(rows, terms)


def angle(first_norms, second_norms, coupling):
    half_gap = 0.5 * (second_norms - first_norms)
    gap_sign = jnp.where(half_gap >= 0.0, 1.0, -1.0)
    denominator = jnp.maximum(
        jnp.abs(half_gap) + jnp.sqrt(half_gap * half_gap + coupling * coupling),
        1e-06 * (first_norms + second_norms),
    )
    tangent = gap_sign * coupling / denominator
    cosine = 1.0 / jnp.sqrt(1.0 + tangent * tangent)
    return cosine, tangent * cosine


def turned_norms(first_norms, second_norms, coupling, cosine, sine):
    new_first = cosine * (cosine * first_norms - sine * coupling) - sine * (cosine * coupling - sine * second_norms)
    new_second = sine * (sine * first_norms + cosine * coupling) + cosine * (sine * coupling + cosine * second_norms)
    return new_first, new_second


def two_rounds(first_norms, second_norms, couplings, gap, keep):
    same, ahead, behind, firsts, seconds = couplings
    cosine, sine = angle(first_norms, second_norms, same)
    new_first, new_second = turned_norms(first_norms, second_norms, same, cosine, sine)
    cosine_gap, sine_gap = left(cosine, gap), left(sine, gap)
    coupling = cosine * (sine_gap * firsts + cosine_gap * ahead) - sine * (sine_gap * behind + cosine_gap * seconds)
    new_second = left(new_second, gap)
    cosine_last, sine_last = angle(new_first, new_second, coupling)
    new_first, new_second = turned_norms(new_first, new_second, coupling, cosine_last, sine_last)
    one, zero = jnp.ones_like(cosine), jnp.zeros_like(cosine)
    turns = (
        jnp.where(keep, one, cosine),
        jnp.where(keep, zero, sine),
        jnp.where(keep, one, cosine_last),
        jnp.where(keep, zero, sine_last),
    )
    return turns, (jnp.where(keep, first_norms, new_first), jnp.where(keep, left(second_norms, gap), new_second))


def joint(x_weights, y_weights, dots, gap):
    total = None
    for a in range(2):
        for b in range(2):
            (x_here, x_gap), (y_here, y_gap) = x_weights[a], y_weights[b]
            before, at, after = [dots[4 * index + 2 * a + b] for index in range(3)]
            part = x_here * (y_here * at + y_gap * after) + x_gap * (y_here * left(before, gap) + y_gap * left(at, gap))
            total = part if total is None else total + part
    return total


def rolled(weights, by):
    return [[left(value, by) for value in pair] for pair in weights]


def load_kernel(offsets_hbm, skip_hbm, loads_hbm, weights_hbm, first_hbm, second_hbm,
                offsets, skip, loads, weights, held, in_sems, out_sems):
    rows = loads.shape[0]
    parts = range(0, rows, BATCH)
    small = [(offsets_hbm, offsets), (skip_hbm, skip), (weights_hbm, weights)]
    large = [(loads_hbm.at[pl.ds(start, BATCH)], loads.at[pl.ds(start, BATCH)]) for start in parts]
    copies = [pltpu.make_async_copy(*ends, in_sems.at[at]) for at, ends in enumerate(small + large)]
    for copy in copies:
        copy.start()
    for copy in copies[:3]:
        copy.wait()
    is_even = (lax.axis_index("pairs") & 1) == 0
    skips = [skip[0, pair].astype(jnp.float32) for pair in range(2)]
    for at, order in enumerate((skips[::-1], skips)):
        held[at, rows:, :] = jnp.full((GROUP, 2 * BLOCK), jnp.where(is_even, *order), jnp.float32)
    weight = [weights[:, block * BLOCK : (block + 1) * BLOCK] for block in range(4)]
    sent = []
    for part, start in enumerate(parts):
        copies[3 + part].wait()
        span = slice(start, start + BATCH)
        blocks = [loads[span, block * BLOCK : (block + 1) * BLOCK] * weight[block] for block in range(4)]
        blocks = blocks[:2] + [left(block, offsets[0, 0]) for block in blocks[2:]]
        last = start + BATCH == rows
        for at, out in enumerate((first_hbm, second_hbm)):
            for half in range(2):
                even, odd = blocks[2 * half + 1 - at], blocks[2 * half + at]
                held[at, span, half * BLOCK : (half + 1) * BLOCK] = jnp.where(is_even, even, odd)
            place = pl.ds(start, BATCH + GROUP if last else BATCH)
            sent.append(pltpu.make_async_copy(held.at[at, place], out.at[place], out_sems.at[at, part]))
            sent[-1].start()
    for copy in sent:
        copy.wait()


def stats_kernel(rows, offsets, first_ref, second_ref, first_out, second_out):
    lags = Lags(offsets, 0)
    for ref, out in ((first_ref, first_out), (second_ref, second_out)):
        store_rows(out, 0, pair_stats(functools.partial(halves, ref), rows, lags))


def cross_kernel(rows, odd_slot, offsets, skip, own_ref, come_ref, end_ref, stats_ref, out_ref):
    is_even = (lax.axis_index("pairs") & 1) == 0
    slot = jnp.where(is_even, 1 - odd_slot, odd_slot)
    lags = Lags(offsets, slot)
    own_first = slot == 1
    is_end = at_end()

    def come(span):
        pair = halves(come_ref, span)
        return pair if odd_slot == 0 else [jnp.where(is_end, a, b) for a, b in zip(halves(end_ref, span), pair)]

    come_stats = pair_stats(come, rows, lags)
    flag_row = slice(rows, rows + 1)
    own_flag, come_flag = halves(own_ref, flag_row)[0], come(flag_row)[0]
    step_flag = jnp.full((1, BLOCK), jnp.where(own_first, skip[1, 1], skip[1, 0]).astype(jnp.float32), jnp.float32)
    own_stats = [stats_ref[index : index + 1, :] for index in range(STATS)]

    def pick(mine, theirs):
        return [jnp.where(own_first, a, b) for a, b in zip(mine, theirs)], [jnp.where(own_first, b, a) for a, b in zip(mine, theirs)]

    for start, stats in zip((0, STATS), pick(own_stats, come_stats)):
        store_rows(out_ref, start, stats)
    for index, lag in enumerate(lags.crossed()):
        sums = sums_over(rows, lambda span: lagged(*pick(halves(own_ref, span), come(span)), lag, lags.gap))
        store_rows(out_ref, CROSS + 12 * index, sums)
    x_flag, y_flag = pick([own_flag], [come_flag])
    store_rows(out_ref, FLAGS, x_flag + y_flag + [step_flag] + [jnp.zeros((1, BLOCK), jnp.float32)] * (SUMS - FLAGS - 3))


def angles_kernel(total_rows, offsets, sums_ref, out_ref):
    lags = Lags(offsets, lax.axis_index("rows") & 1)
    rows = [sums_ref[index : index + 1, :] for index in range(FLAGS + 3)]
    sides = []
    for side, is_low in ((0, lags.x_low), (1, jnp.logical_not(lags.y_up))):
        stats = rows[side * STATS : (side + 1) * STATS]
        (cosine, sine, cosine_last, sine_last), norms = two_rounds(stats[0], stats[1], stats[2:7], lags.gap, rows[FLAGS + side] > 0.5)
        here = jnp.where(is_low, sine_last, cosine_last)
        ahead = jnp.where(is_low, cosine_last, -sine_last)
        weights = [
            [here * cosine, ahead * left(sine, lags.gap)],
            [-here * sine, ahead * left(cosine, lags.gap)],
        ]
        sides.append((jnp.where(is_low, norms[1], norms[0]), weights, stats[7:], [cosine, sine, here, ahead]))
    (x_norms, x_weights, x_dots, x_turns), (y_norms, y_weights, y_dots, y_turns) = sides
    crossed = [
        joint(x_weights, rolled(y_weights, lag), rows[CROSS + 12 * index : CROSS + 12 * (index + 1)], lags.gap)
        for index, lag in enumerate(lags.crossed())
    ]
    firsts = joint(x_weights, rolled(x_weights, lags.turn), x_dots, lags.gap)
    seconds = left(joint(y_weights, rolled(y_weights, lags.turn), y_dots, lags.gap), lags.lag)
    couplings = (crossed[0], crossed[1], left(crossed[2], lags.turn), firsts, seconds)
    turns, (upper, lower) = two_rounds(x_norms, left(y_norms, lags.lag), couplings, lags.turn, rows[FLAGS + 2] > 0.5)
    norms = [right(upper, lags.x_shift) / total_rows, right(lower, lags.out) / total_rows]
    store_rows(out_ref, 0, x_turns + y_turns + list(turns) + norms + [jnp.zeros_like(upper)] * (ANGLES - NORMS - 2))


def turn(x, y, cosine, sine):
    return cosine * x - sine * y, sine * x + cosine * y


def block_after(pair, turns, gap):
    cosine, sine, here, ahead = turns
    upper, lower = turn(*pair, cosine, sine)
    return here * upper + ahead * left(lower, gap)


def last_kernel(offsets, mine_ref, other_ref, first_ref, second_ref, first_come, second_come,
                rotated_hbm, power_hbm, rotated, power, sems):
    rows = rotated.shape[0]
    is_even = (lax.axis_index("pairs") & 1) == 0
    on_first_core = (lax.axis_index("rows") & 1) == 0
    mine, other = mine_ref[...], other_ref[...]
    is_end = at_end()

    def pair_at(ref, span):
        pair = halves(ref, span)
        return [jnp.where(is_end, a, b) for a, b in zip(halves(second_ref, span), pair)] if ref is second_come else pair

    sources = (((second_come, first_come), (first_ref, second_ref)), ((second_ref, first_ref), (first_come, second_come)))
    slots = [jnp.where(on_first_core, mine, other), jnp.where(on_first_core, other, mine)]
    for slot in range(2):
        for half in range(2):
            at = 2 * half + slot
            power[:, at * BLOCK : (at + 1) * BLOCK] = slots[slot][NORMS + half : NORMS + half + 1]
    copies = [pltpu.make_async_copy(power, power_hbm, sems.at[4])]
    copies[0].start()
    for slot, angles in enumerate(slots):
        lags = Lags(offsets, slot)
        blocks = [slice(at * BLOCK, (at + 1) * BLOCK) for at in (slot, 2 + slot)]
        turns = [angles[index : index + 1] for index in range(NORMS)]
        for start in range(0, rows, BATCH):
            span = slice(start, start + BATCH)
            x, y = [
                [jnp.where(is_even, a, b) for a, b in zip(pair_at(even_ref, span), pair_at(odd_ref, span))]
                for even_ref, odd_ref in sources[slot]
            ]
            upper = block_after(x, turns[:4], lags.gap)
            lower = left(block_after(y, turns[4:8], lags.gap), lags.lag)
            upper, lower = turn(upper, lower, turns[8], turns[9])
            upper, lower = turn(upper, left(lower, lags.turn), turns[10], turns[11])
            rotated[span, blocks[0]] = right(upper, lags.x_shift) if slot else upper
            rotated[span, blocks[1]] = right(lower, lags.out)
        for half, columns in enumerate(blocks):
            copies.append(pltpu.make_async_copy(rotated.at[:, columns], rotated_hbm.at[:, columns], sems.at[2 * slot + half]))
            copies[-1].start()
    for copy in copies:
        copy.wait()


VMEM = pl.BlockSpec(memory_space=pltpu.VMEM)
HBM = pl.BlockSpec(memory_space=pltpu.HBM)


def call(kernel, operands, outs, name, scratch=(), micros=1, grant=VMEM_LIMIT):
    return pl.pallas_call(
        kernel,
        out_shape=[jax.ShapeDtypeStruct(shape, jnp.float32) for shape, _ in outs],
        in_specs=[space for _, space in operands],
        out_specs=[space for _, space in outs],
        scratch_shapes=scratch,
        name=name,
        cost_estimate=pl.CostEstimate(flops=micros * 10**9, bytes_accessed=micros * 10**6, transcendentals=0),
        compiler_params=pltpu.CompilerParams(vmem_limit_bytes=grant),
    )(*[array for array, _ in operands])


def swap_rows(x, partner):
    size = lax.axis_size("rows")
    depth = size // 4

    def other(row):
        y, z, core = partner(row // (2 * depth), (row // 2) % depth, row % 2)
        return (y * depth + z) * 2 + core

    return lax.ppermute(x, "rows", [(row, other(row)) for row in range(size)])


OPPOSITE = (6, 7, 4, 5, 2, 3, 0, 1)


def per_device(loads, col_weights, partner_offsets, skip_mask):
    rows, columns = loads.shape
    pairs = lax.axis_size("pairs")
    weights = col_weights.reshape(1, columns)
    held = (rows + GROUP, 2 * BLOCK)
    first, second = call(
        load_kernel,
        [(partner_offsets, HBM), (skip_mask, HBM), (loads, HBM), (weights, HBM)],
        [(held, HBM)] * 2,
        "load",
        [
            pltpu.VMEM(partner_offsets.shape, jnp.int32),
            pltpu.VMEM(skip_mask.shape, jnp.int32),
            pltpu.VMEM((rows, columns), jnp.float32),
            pltpu.VMEM((1, columns), jnp.float32),
            pltpu.VMEM((2,) + held, jnp.float32),
            pltpu.SemaphoreType.DMA((3 + rows // BATCH,)),
            pltpu.SemaphoreType.DMA((2, rows // BATCH)),
        ],
        grant=None,
    )
    second_come = lax.ppermute(second, "pairs", [(at, (((at + 1) ^ 1) - 1) % pairs) for at in range(pairs)])
    first_come = lax.ppermute(first, "pairs", [(at, at ^ 1) for at in range(pairs)])
    offsets, skips = (partner_offsets, VMEM), (skip_mask, VMEM)
    first_stats, second_stats = call(
        functools.partial(stats_kernel, rows), [offsets, (first, VMEM), (second, VMEM)], [((24, BLOCK), VMEM)] * 2, "stats"
    )
    slots = []
    for odd_slot, own, come, stats in ((0, second, first_come, second_stats), (1, first, second_come, first_stats)):
        slots += call(
            functools.partial(cross_kernel, rows, odd_slot),
            [offsets, skips, (own, VMEM), (come, VMEM), (second, VMEM), (stats, VMEM)],
            [((SUMS, BLOCK), VMEM)],
            "cross",
        )
    keeps_first = (lax.axis_index("pairs") & 1) == (lax.axis_index("rows") & 1)
    sums = jnp.where(keeps_first, slots[1], slots[0])
    sums = sums + swap_rows(jnp.where(keeps_first, slots[0], slots[1]), lambda y, z, core: (y, z, 1 - core))
    sums = sums + swap_rows(sums, lambda y, z, core: (1 - y, z, core))
    near = [swap_rows(sums, lambda y, z, core, by=by: (y, z ^ by, core)) for by in (1, 2, 3)]
    sums = (sums + near[0]) + (near[1] + near[2])
    sums = sums + swap_rows(sums, lambda y, z, core: (y, OPPOSITE[z], core))
    total_rows = float(rows * lax.axis_size("rows"))
    (angles,) = call(functools.partial(angles_kernel, total_rows), [offsets, (sums, VMEM)], [((ANGLES, BLOCK), VMEM)], "angles")
    other = swap_rows(angles, lambda y, z, core: (y, z, 1 - core))
    rotated, power = call(
        last_kernel,
        [offsets] + [(array, VMEM) for array in (angles, other, first, second, first_come, second_come)],
        [((rows, columns), HBM), ((1, columns), HBM)],
        "last",
        [pltpu.VMEM((rows, columns), jnp.float32), pltpu.VMEM((1, columns), jnp.float32), pltpu.SemaphoreType.DMA((5,))],
    )
    return rotated, power.reshape(columns)


def solution(mesh):
    in_specs = (P("rows", "pairs"), P("pairs"), P(), P(None, "pairs"))
    out_specs = (P("rows", "pairs"), P("pairs"))
    return jax.shard_map(
        per_device, mesh=mesh, in_specs=in_specs, out_specs=out_specs, check_vma=False
    )
```

```python
import functools
import jax
import jax.numpy as jnp
from jax import lax
from jax.experimental import pallas as pl
from jax.experimental.pallas import tpu as pltpu
from jax.sharding import PartitionSpec as P

BLOCK = 128
GROUP = 8
BATCH = 128

STATS = 19
CROSS = 2 * STATS
FLAGS = CROSS + 36
SUMS = 80
SIDE = 24
NORMS = 12
ANGLES = 16
VMEM_LIMIT = 8 * 1024 * 1024


def left(x, by):
    return pltpu.roll(x, (-by) & (BLOCK - 1), 1)


def right(x, by):
    return pltpu.roll(x, by & (BLOCK - 1), 1)


def at_end():
    place = lax.axis_index("pairs")
    return (place == 0) | (place == lax.axis_size("pairs") - 1)


def kept_slot():
    row = lax.axis_index("rows")
    return (row ^ (row >> 1) ^ (row >> 2) ^ (row >> 4)) & 1


class Lags:
    def __init__(self, offsets, slot):
        place = lax.axis_index("pairs")
        self.first = offsets[0, 0]
        self.gap = offsets[0, 1] - offsets[0, 0]
        self.turn = offsets[1, 1] - offsets[1, 0]
        self.x_low = (slot == 1) & (place == 0)
        self.y_up = (slot == 1) & (place == lax.axis_size("pairs") - 1)
        self.x_shift = jnp.where(self.x_low, offsets[0, 1], 0)
        y_shift = jnp.where(self.y_up, 0, offsets[0, 1])
        self.lag = offsets[1, 0] - y_shift + self.x_shift
        self.out = self.x_shift + offsets[1, 1]

    def crossed(self):
        return (self.lag, self.lag + self.turn, self.lag - self.turn)


def halves(ref, span):
    return ref[span, :BLOCK], ref[span, BLOCK:]


def sums_over(rows, terms):
    totals = None
    for start in range(0, rows, BATCH):
        parts = [jnp.sum(term.reshape(BATCH // GROUP, GROUP, BLOCK), axis=0) for term in terms(slice(start, start + BATCH))]
        totals = parts if totals is None else [total + part for total, part in zip(totals, parts)]
    return [jnp.sum(total, axis=0, keepdims=True) for total in totals]


def store_rows(out_ref, start, values):
    for index, value in enumerate(values):
        out_ref[start + index : start + index + 1, :] = value


def lagged(x, y, lag, gap):
    terms = []
    for by in (lag - gap, lag, lag + gap):
        moved = [left(half, by) for half in y]
        terms += [a * b for a in x for b in moved]
    return terms


def pair_stats(ref, lags):
    def terms(span):
        upper, lower = halves(ref, span)
        upper_gap, lower_gap = left(upper, lags.gap), left(lower, lags.gap)
        step_0 = [upper * upper, lower * lower, upper * lower, upper * lower_gap, upper_gap * lower, upper * upper_gap, lower * lower_gap]
        return step_0 + lagged((upper, lower), (upper, lower), lags.turn, lags.gap)

    return sums_over(ref.shape[0], terms)


def angle(first_norms, second_norms, coupling):
    half_gap = 0.5 * (second_norms - first_norms)
    gap_sign = jnp.where(half_gap >= 0.0, 1.0, -1.0)
    denominator = jnp.maximum(
        jnp.abs(half_gap) + jnp.sqrt(half_gap * half_gap + coupling * coupling),
        1e-06 * (first_norms + second_norms),
    )
    tangent = gap_sign * coupling / denominator
    cosine = 1.0 / jnp.sqrt(1.0 + tangent * tangent)
    return cosine, tangent * cosine


def turned_norms(first_norms, second_norms, coupling, cosine, sine):
    new_first = cosine * (cosine * first_norms - sine * coupling) - sine * (cosine * coupling - sine * second_norms)
    new_second = sine * (sine * first_norms + cosine * coupling) + cosine * (sine * coupling + cosine * second_norms)
    return new_first, new_second


def two_rounds(first_norms, second_norms, couplings, gap, keep):
    same, ahead, behind, firsts, seconds = couplings
    cosine, sine = angle(first_norms, second_norms, same)
    new_first, new_second = turned_norms(first_norms, second_norms, same, cosine, sine)
    cosine_gap, sine_gap = left(cosine, gap), left(sine, gap)
    coupling = cosine * (sine_gap * firsts + cosine_gap * ahead) - sine * (sine_gap * behind + cosine_gap * seconds)
    new_second = left(new_second, gap)
    cosine_last, sine_last = angle(new_first, new_second, coupling)
    new_first, new_second = turned_norms(new_first, new_second, coupling, cosine_last, sine_last)
    one, zero = jnp.ones_like(cosine), jnp.zeros_like(cosine)
    turns = (
        jnp.where(keep, one, cosine),
        jnp.where(keep, zero, sine),
        jnp.where(keep, one, cosine_last),
        jnp.where(keep, zero, sine_last),
    )
    return turns, (jnp.where(keep, first_norms, new_first), jnp.where(keep, left(second_norms, gap), new_second))


def joint(x_weights, y_weights, dots, gap):
    total = None
    for a in range(2):
        for b in range(2):
            (x_here, x_gap), (y_here, y_gap) = x_weights[a], y_weights[b]
            before, at, after = [dots[4 * index + 2 * a + b] for index in range(3)]
            part = x_here * (y_here * at + y_gap * after) + x_gap * (y_here * left(before, gap) + y_gap * left(at, gap))
            total = part if total is None else total + part
    return total


def rolled(weights, by):
    return [[left(value, by) for value in pair] for pair in weights]


def align_into(out_ref, raw, weights, lags):
    for start in range(0, out_ref.shape[0], BATCH):
        span = slice(start, start + BATCH)
        upper, lower = raw(span)
        out_ref[span, :BLOCK] = upper * weights[0]
        out_ref[span, BLOCK:] = left(lower, lags.first) * weights[1]


def own_kernel(offsets, skip, weights_ref, first_raw, second_raw, first_ref, second_ref, first_side, second_side):
    lags = Lags(offsets, 0)
    is_even = (lax.axis_index("pairs") & 1) == 0
    weights = [weights_ref[:, block * BLOCK : (block + 1) * BLOCK] for block in range(4)]
    skips = [skip[0, pair].astype(jnp.float32) for pair in range(2)]
    for even, raw_ref, ref, side in ((1, first_raw, first_ref, first_side), (0, second_raw, second_ref, second_side)):
        odd = 1 - even
        weight = [jnp.where(is_even, weights[2 * half + even], weights[2 * half + odd]) for half in range(2)]
        weight[1] = left(weight[1], lags.first)
        align_into(ref, functools.partial(halves, raw_ref), weight, lags)
        flag = jnp.full((1, BLOCK), jnp.where(is_even, skips[even], skips[odd]), jnp.float32)
        rows = pair_stats(ref, lags) + weight + [flag]
        store_rows(side, 0, rows + [jnp.zeros_like(flag)] * (SIDE - len(rows)))


def cross_kernel(odd_slot, offsets, skip, own_ref, own_side, raw_ref, come_side, end_ref, end_side, out_ref, come_ref):
    is_even = (lax.axis_index("pairs") & 1) == 0
    slot = jnp.where(is_even, 1 - odd_slot, odd_slot)
    lags = Lags(offsets, slot)
    own_first = slot == 1
    rows = range(STATS + 3)
    own = [own_side[row : row + 1, :] for row in rows]
    come = [come_side[row : row + 1, :] for row in rows]
    align_into(come_ref, functools.partial(halves, raw_ref), come[STATS : STATS + 2], lags)
    if odd_slot == 1:

        @pl.when(at_end())
        def _():
            come_ref[...] = end_ref[...]

        come = [jnp.where(at_end(), end_side[row : row + 1, :], value) for row, value in zip(rows, come)]
    step_flag = jnp.full((1, BLOCK), jnp.where(own_first, skip[1, 1], skip[1, 0]).astype(jnp.float32), jnp.float32)

    def pick(mine, theirs):
        return [jnp.where(own_first, a, b) for a, b in zip(mine, theirs)], [jnp.where(own_first, b, a) for a, b in zip(mine, theirs)]

    x_side, y_side = pick(own, come)
    store_rows(out_ref, 0, x_side[:STATS] + y_side[:STATS])
    for index, lag in enumerate(lags.crossed()):

        def terms(span):
            x, y = pick(halves(own_ref, span), halves(come_ref, span))
            return lagged(x, y, lag, lags.gap)

        store_rows(out_ref, CROSS + 12 * index, sums_over(own_ref.shape[0], terms))
    store_rows(out_ref, FLAGS, x_side[-1:] + y_side[-1:] + [step_flag] + [jnp.zeros_like(step_flag)] * (SUMS - FLAGS - 3))


def angles_kernel(total_rows, offsets, sums_ref, out_ref):
    lags = Lags(offsets, kept_slot())
    rows = [sums_ref[index : index + 1, :] for index in range(FLAGS + 3)]
    sides = []
    for side, is_low in ((0, lags.x_low), (1, jnp.logical_not(lags.y_up))):
        stats = rows[side * STATS : (side + 1) * STATS]
        (cosine, sine, cosine_last, sine_last), norms = two_rounds(stats[0], stats[1], stats[2:7], lags.gap, rows[FLAGS + side] > 0.5)
        here = jnp.where(is_low, sine_last, cosine_last)
        ahead = jnp.where(is_low, cosine_last, -sine_last)
        weights = [
            [here * cosine, ahead * left(sine, lags.gap)],
            [-here * sine, ahead * left(cosine, lags.gap)],
        ]
        sides.append((jnp.where(is_low, norms[1], norms[0]), weights, stats[7:], [cosine, sine, here, ahead]))
    (x_norms, x_weights, x_dots, x_turns), (y_norms, y_weights, y_dots, y_turns) = sides
    crossed = [
        joint(x_weights, rolled(y_weights, lag), rows[CROSS + 12 * index : CROSS + 12 * (index + 1)], lags.gap)
        for index, lag in enumerate(lags.crossed())
    ]
    firsts = joint(x_weights, rolled(x_weights, lags.turn), x_dots, lags.gap)
    seconds = left(joint(y_weights, rolled(y_weights, lags.turn), y_dots, lags.gap), lags.lag)
    couplings = (crossed[0], crossed[1], left(crossed[2], lags.turn), firsts, seconds)
    turns, (upper, lower) = two_rounds(x_norms, left(y_norms, lags.lag), couplings, lags.turn, rows[FLAGS + 2] > 0.5)
    norms = [right(upper, lags.x_shift) / total_rows, right(lower, lags.out) / total_rows]
    store_rows(out_ref, 0, x_turns + y_turns + list(turns) + norms + [jnp.zeros_like(upper)] * (ANGLES - NORMS - 2))


def turn(x, y, cosine, sine):
    return cosine * x - sine * y, sine * x + cosine * y


def block_after(pair, turns, gap):
    cosine, sine, here, ahead = turns
    upper, lower = turn(*pair, cosine, sine)
    return here * upper + ahead * left(lower, gap)


def last_kernel(offsets, mine_ref, other_ref, first_ref, second_ref, first_come, second_come,
                rotated_hbm, power_hbm, rotated, power, sems):
    rows = rotated.shape[0]
    is_even = (lax.axis_index("pairs") & 1) == 0
    keeps_first = kept_slot() == 0
    mine, other = mine_ref[...], other_ref[...]
    sources = (((second_come, first_come), (first_ref, second_ref)), ((second_ref, first_ref), (first_come, second_come)))
    slots = [jnp.where(keeps_first, mine, other), jnp.where(keeps_first, other, mine)]
    for slot in range(2):
        for half in range(2):
            at = 2 * half + slot
            power[:, at * BLOCK : (at + 1) * BLOCK] = slots[slot][NORMS + half : NORMS + half + 1]
    copies = [pltpu.make_async_copy(power, power_hbm, sems.at[4])]
    copies[0].start()
    for slot, angles in enumerate(slots):
        lags = Lags(offsets, slot)
        blocks = [slice(at * BLOCK, (at + 1) * BLOCK) for at in (slot, 2 + slot)]
        turns = [angles[index : index + 1] for index in range(NORMS)]
        for start in range(0, rows, BATCH):
            span = slice(start, start + BATCH)
            x, y = [
                [jnp.where(is_even, a, b) for a, b in zip(halves(even_ref, span), halves(odd_ref, span))]
                for even_ref, odd_ref in sources[slot]
            ]
            upper = block_after(x, turns[:4], lags.gap)
            lower = left(block_after(y, turns[4:8], lags.gap), lags.lag)
            upper, lower = turn(upper, lower, turns[8], turns[9])
            upper, lower = turn(upper, left(lower, lags.turn), turns[10], turns[11])
            rotated[span, blocks[0]] = right(upper, lags.x_shift) if slot else upper
            rotated[span, blocks[1]] = right(lower, lags.out)
        for half, columns in enumerate(blocks):
            copies.append(pltpu.make_async_copy(rotated.at[:, columns], rotated_hbm.at[:, columns], sems.at[2 * slot + half]))
            copies[-1].start()
    for copy in copies:
        copy.wait()


VMEM = pl.BlockSpec(memory_space=pltpu.VMEM)
HBM = pl.BlockSpec(memory_space=pltpu.HBM)


def call(kernel, operands, outs, name, scratch=(), micros=1, grant=VMEM_LIMIT):
    return pl.pallas_call(
        kernel,
        out_shape=[jax.ShapeDtypeStruct(shape, jnp.float32) for shape, _ in outs],
        in_specs=[space for _, space in operands],
        out_specs=[space for _, space in outs],
        scratch_shapes=scratch,
        name=name,
        cost_estimate=pl.CostEstimate(flops=micros * 10**9, bytes_accessed=micros * 10**6, transcendentals=0),
        compiler_params=pltpu.CompilerParams(vmem_limit_bytes=grant),
    )(*[array for array, _ in operands])


def swap_rows(x, partner):
    size = lax.axis_size("rows")
    depth = size // 4

    def other(row):
        y, z, core = partner(row // (2 * depth), (row // 2) % depth, row % 2)
        return (y * depth + z) * 2 + core

    return lax.ppermute(x, "rows", [(row, other(row)) for row in range(size)])


OPPOSITE = (6, 7, 4, 5, 2, 3, 0, 1)


def per_device(loads, col_weights, partner_offsets, skip_mask):
    rows, columns = loads.shape
    pairs = lax.axis_size("pairs")
    weights = (col_weights.reshape(1, columns), VMEM)
    offsets, skips = (partner_offsets, VMEM), (skip_mask, VMEM)
    is_even = (lax.axis_index("pairs") & 1) == 0
    blocks = [loads[:, at * BLOCK : (at + 1) * BLOCK] for at in range(4)]
    raw = [
        jnp.concatenate([jnp.where(is_even, blocks[even + at], blocks[1 - even + at]) for at in (0, 2)], axis=1) for even in (1, 0)
    ]

    def swap_first(x):
        return lax.ppermute(x, "pairs", [(at, at ^ 1) for at in range(pairs)])

    def swap_second(x):
        return lax.ppermute(x, "pairs", [(at, (((at + 1) ^ 1) - 1) % pairs) for at in range(pairs)])

    pair, side = ((rows, 2 * BLOCK), VMEM), ((SIDE, BLOCK), VMEM)
    second_raw = swap_second(raw[1])
    first_raw = swap_first(raw[0])
    first, second, first_side, second_side = [
        (array, VMEM)
        for array in call(own_kernel, [offsets, skips, weights] + [(array, VMEM) for array in raw], [pair, pair, side, side], "own")
    ]
    slots, come = [], []
    for odd_slot, own, own_side, raw_come, side_come in (
        (0, second, second_side, first_raw, swap_first(first_side[0])),
        (1, first, first_side, second_raw, swap_second(second_side[0])),
    ):
        sums, aligned = call(
            functools.partial(cross_kernel, odd_slot),
            [offsets, skips, own, own_side, (raw_come, VMEM), (side_come, VMEM), second, second_side],
            [((SUMS, BLOCK), VMEM), pair],
            "cross",
        )
        slots.append(sums)
        come.append((aligned, VMEM))
    keeps_first = (lax.axis_index("pairs") & 1) == kept_slot()
    sums = jnp.where(keeps_first, slots[1], slots[0])
    sums = sums + swap_rows(jnp.where(keeps_first, slots[0], slots[1]), lambda y, z, core: (y, z, 1 - core))
    sums = sums + swap_rows(sums, lambda y, z, core: (1 - y, z, 1 - core))
    near = [swap_rows(sums, lambda y, z, core, by=by: (y, z ^ by, core if by == 3 else 1 - core)) for by in (3, 2, 1)]
    sums = (sums + near[0]) + (near[1] + near[2])
    sums = sums + swap_rows(sums, lambda y, z, core: (y, OPPOSITE[z], 1 - core))
    total_rows = float(rows * lax.axis_size("rows"))
    (angles,) = call(functools.partial(angles_kernel, total_rows), [offsets, (sums, VMEM)], [((ANGLES, BLOCK), VMEM)], "angles")
    other = swap_rows(angles, lambda y, z, core: (y, z, 1 - core))
    rotated, power = call(
        last_kernel,
        [offsets, (angles, VMEM), (other, VMEM), first, second] + come,
        [((rows, columns), HBM), ((1, columns), HBM)],
        "last",
        [pltpu.VMEM((rows, columns), jnp.float32), pltpu.VMEM((1, columns), jnp.float32), pltpu.SemaphoreType.DMA((5,))],
    )
    return rotated, power.reshape(columns)


def solution(mesh):
    in_specs = (P("rows", "pairs"), P("pairs"), P(), P(None, "pairs"))
    out_specs = (P("rows", "pairs"), P("pairs"))
    return jax.shard_map(
        per_device, mesh=mesh, in_specs=in_specs, out_specs=out_specs, check_vma=False
    )
```

```python
import functools
import jax
import jax.numpy as jnp
from jax import lax
from jax.experimental import pallas as pl
from jax.experimental.pallas import tpu as pltpu
from jax.sharding import PartitionSpec as P

BLOCK = 128
GROUP = 8
BATCH = 128

STATS = 19
CROSS = 2 * STATS
FLAGS = CROSS + 36
SUMS = 80
SIDE = 24
NORMS = 12
ANGLES = 16
VMEM_LIMIT = 8 * 1024 * 1024


def left(x, by):
    return pltpu.roll(x, (-by) & (BLOCK - 1), 1)


def right(x, by):
    return pltpu.roll(x, by & (BLOCK - 1), 1)


def at_end():
    place = lax.axis_index("pairs")
    return (place == 0) | (place == lax.axis_size("pairs") - 1)


def kept_slot():
    row = lax.axis_index("rows")
    return (row ^ (row >> 1) ^ (row >> 2) ^ (row >> 4)) & 1


class Lags:
    def __init__(self, offsets, slot):
        place = lax.axis_index("pairs")
        self.first = offsets[0, 0]
        self.gap = offsets[0, 1] - offsets[0, 0]
        self.turn = offsets[1, 1] - offsets[1, 0]
        self.x_low = (slot == 1) & (place == 0)
        self.y_up = (slot == 1) & (place == lax.axis_size("pairs") - 1)
        self.x_shift = jnp.where(self.x_low, offsets[0, 1], 0)
        y_shift = jnp.where(self.y_up, 0, offsets[0, 1])
        self.lag = offsets[1, 0] - y_shift + self.x_shift
        self.out = self.x_shift + offsets[1, 1]

    def crossed(self):
        return (self.lag, self.lag + self.turn, self.lag - self.turn)


def halves(ref, span):
    return ref[span, :BLOCK], ref[span, BLOCK:]


def sums_over(rows, terms):
    totals = None
    for start in range(0, rows, BATCH):
        parts = [jnp.sum(term.reshape(BATCH // GROUP, GROUP, BLOCK), axis=0) for term in terms(slice(start, start + BATCH))]
        totals = parts if totals is None else [total + part for total, part in zip(totals, parts)]
    return [jnp.sum(total, axis=0, keepdims=True) for total in totals]


def store_rows(out_ref, start, values):
    for index, value in enumerate(values):
        out_ref[start + index : start + index + 1, :] = value


def moved_by_gap(x, lags):
    return [left(half, lags.gap) for half in x], x, [right(half, lags.gap) for half in x]


def lagged(x_moved, y, lag):
    ahead = [left(half, lag) for half in y]
    return [a * b for x in x_moved for a in x for b in ahead]


def pair_stats(ref, lags):
    def terms(span):
        pair = halves(ref, span)
        moved = moved_by_gap(pair, lags)
        (upper, lower), (upper_gap, lower_gap) = pair, moved[0]
        step_0 = [upper * upper, lower * lower, upper * lower, upper * lower_gap, upper_gap * lower, upper * upper_gap, lower * lower_gap]
        return step_0 + lagged(moved, pair, lags.turn)

    return sums_over(ref.shape[0], terms)


def angle(first_norms, second_norms, coupling):
    half_gap = 0.5 * (second_norms - first_norms)
    gap_sign = jnp.where(half_gap >= 0.0, 1.0, -1.0)
    denominator = jnp.maximum(
        jnp.abs(half_gap) + jnp.sqrt(half_gap * half_gap + coupling * coupling),
        1e-06 * (first_norms + second_norms),
    )
    tangent = gap_sign * coupling / denominator
    cosine = 1.0 / jnp.sqrt(1.0 + tangent * tangent)
    return cosine, tangent * cosine


def turned_norms(first_norms, second_norms, coupling, cosine, sine):
    new_first = cosine * (cosine * first_norms - sine * coupling) - sine * (cosine * coupling - sine * second_norms)
    new_second = sine * (sine * first_norms + cosine * coupling) + cosine * (sine * coupling + cosine * second_norms)
    return new_first, new_second


def two_rounds(first_norms, second_norms, couplings, gap, keep):
    same, ahead, behind, firsts, seconds = couplings
    cosine, sine = angle(first_norms, second_norms, same)
    new_first, new_second = turned_norms(first_norms, second_norms, same, cosine, sine)
    cosine_gap, sine_gap = left(cosine, gap), left(sine, gap)
    coupling = cosine * (sine_gap * firsts + cosine_gap * ahead) - sine * (sine_gap * behind + cosine_gap * seconds)
    new_second = left(new_second, gap)
    cosine_last, sine_last = angle(new_first, new_second, coupling)
    new_first, new_second = turned_norms(new_first, new_second, coupling, cosine_last, sine_last)
    one, zero = jnp.ones_like(cosine), jnp.zeros_like(cosine)
    turns = (
        jnp.where(keep, one, cosine),
        jnp.where(keep, zero, sine),
        jnp.where(keep, one, cosine_last),
        jnp.where(keep, zero, sine_last),
    )
    return turns, (jnp.where(keep, first_norms, new_first), jnp.where(keep, left(second_norms, gap), new_second))


def joint(x_weights, y_weights, dots, gap):
    total = None
    for a in range(2):
        for b in range(2):
            (x_here, x_gap), (y_here, y_gap) = x_weights[a], y_weights[b]
            before, at, after = [dots[4 * index + 2 * a + b] for index in range(3)]
            part = x_here * (y_here * at + y_gap * left(after, gap)) + x_gap * (y_here * before + y_gap * left(at, gap))
            total = part if total is None else total + part
    return total


def rolled(weights, by):
    return [[left(value, by) for value in pair] for pair in weights]


def align_into(out_ref, raw, weights, lags):
    for start in range(0, out_ref.shape[0], BATCH):
        span = slice(start, start + BATCH)
        upper, lower = raw(span)
        out_ref[span, :BLOCK] = upper * weights[0]
        out_ref[span, BLOCK:] = left(lower, lags.first) * weights[1]


def own_kernel(offsets, skip, weights_ref, first_raw, second_raw, first_ref, second_ref, first_side, second_side):
    lags = Lags(offsets, 0)
    is_even = (lax.axis_index("pairs") & 1) == 0
    weights = [weights_ref[:, block * BLOCK : (block + 1) * BLOCK] for block in range(4)]
    skips = [skip[0, pair].astype(jnp.float32) for pair in range(2)]
    for even, raw_ref, ref, side in ((1, first_raw, first_ref, first_side), (0, second_raw, second_ref, second_side)):
        odd = 1 - even
        weight = [jnp.where(is_even, weights[2 * half + even], weights[2 * half + odd]) for half in range(2)]
        weight[1] = left(weight[1], lags.first)
        align_into(ref, functools.partial(halves, raw_ref), weight, lags)
        flag = jnp.full((1, BLOCK), jnp.where(is_even, skips[even], skips[odd]), jnp.float32)
        rows = pair_stats(ref, lags) + weight + [flag]
        store_rows(side, 0, rows + [jnp.zeros_like(flag)] * (SIDE - len(rows)))


def cross_kernel(odd_slot, offsets, skip, own_ref, own_side, raw_ref, come_side, end_ref, end_side, _, out_ref, come_ref, moved_ref):
    is_even = (lax.axis_index("pairs") & 1) == 0
    slot = jnp.where(is_even, 1 - odd_slot, odd_slot)
    lags = Lags(offsets, slot)
    own_first = slot == 1
    rows = range(STATS + 3)
    own = [own_side[row : row + 1, :] for row in rows]
    come = [come_side[row : row + 1, :] for row in rows]
    align_into(come_ref, functools.partial(halves, raw_ref), come[STATS : STATS + 2], lags)
    if odd_slot == 1:

        @pl.when(at_end())
        def _():
            come_ref[...] = end_ref[...]

        come = [jnp.where(at_end(), end_side[row : row + 1, :], value) for row, value in zip(rows, come)]
    step_flag = jnp.full((1, BLOCK), jnp.where(own_first, skip[1, 1], skip[1, 0]).astype(jnp.float32), jnp.float32)

    def pick(mine, theirs):
        return [jnp.where(own_first, a, b) for a, b in zip(mine, theirs)], [jnp.where(own_first, b, a) for a, b in zip(mine, theirs)]

    x_side, y_side = pick(own, come)
    store_rows(out_ref, 0, x_side[:STATS] + y_side[:STATS])
    for start in range(0, own_ref.shape[0], BATCH):
        span = slice(start, start + BATCH)
        x, _ = pick(halves(own_ref, span), halves(come_ref, span))
        for at, half in enumerate(half for pair in moved_by_gap(x, lags) for half in pair):
            moved_ref[span, at * BLOCK : (at + 1) * BLOCK] = half
    for index, lag in enumerate(lags.crossed()):

        def terms(span):
            _, y = pick(halves(own_ref, span), halves(come_ref, span))
            moved = [[moved_ref[span, at * BLOCK : (at + 1) * BLOCK] for at in (two, two + 1)] for two in (0, 2, 4)]
            return lagged(moved, y, lag)

        store_rows(out_ref, CROSS + 12 * index, sums_over(own_ref.shape[0], terms))
    store_rows(out_ref, FLAGS, x_side[-1:] + y_side[-1:] + [step_flag] + [jnp.zeros_like(step_flag)] * (SUMS - FLAGS - 3))


def angles_kernel(total_rows, offsets, sums_ref, out_ref):
    lags = Lags(offsets, kept_slot())
    rows = [sums_ref[index : index + 1, :] for index in range(FLAGS + 3)]
    sides = []
    for side, is_low in ((0, lags.x_low), (1, jnp.logical_not(lags.y_up))):
        stats = rows[side * STATS : (side + 1) * STATS]
        (cosine, sine, cosine_last, sine_last), norms = two_rounds(stats[0], stats[1], stats[2:7], lags.gap, rows[FLAGS + side] > 0.5)
        here = jnp.where(is_low, sine_last, cosine_last)
        ahead = jnp.where(is_low, cosine_last, -sine_last)
        weights = [
            [here * cosine, ahead * left(sine, lags.gap)],
            [-here * sine, ahead * left(cosine, lags.gap)],
        ]
        sides.append((jnp.where(is_low, norms[1], norms[0]), weights, stats[7:], [cosine, sine, here, ahead]))
    (x_norms, x_weights, x_dots, x_turns), (y_norms, y_weights, y_dots, y_turns) = sides
    crossed = [
        joint(x_weights, rolled(y_weights, lag), rows[CROSS + 12 * index : CROSS + 12 * (index + 1)], lags.gap)
        for index, lag in enumerate(lags.crossed())
    ]
    firsts = joint(x_weights, rolled(x_weights, lags.turn), x_dots, lags.gap)
    seconds = left(joint(y_weights, rolled(y_weights, lags.turn), y_dots, lags.gap), lags.lag)
    couplings = (crossed[0], crossed[1], left(crossed[2], lags.turn), firsts, seconds)
    turns, (upper, lower) = two_rounds(x_norms, left(y_norms, lags.lag), couplings, lags.turn, rows[FLAGS + 2] > 0.5)
    norms = [right(upper, lags.x_shift) / total_rows, right(lower, lags.out) / total_rows]
    store_rows(out_ref, 0, x_turns + y_turns + list(turns) + norms + [jnp.zeros_like(upper)] * (ANGLES - NORMS - 2))


def turn(x, y, cosine, sine):
    return cosine * x - sine * y, sine * x + cosine * y


def block_after(pair, turns, gap):
    cosine, sine, here, ahead = turns
    upper, lower = turn(*pair, cosine, sine)
    return here * upper + ahead * left(lower, gap)


def last_kernel(offsets, mine_ref, other_ref, first_ref, second_ref, first_come, second_come,
                rotated_hbm, power_hbm, rotated, power, sems):
    rows = rotated.shape[0]
    is_even = (lax.axis_index("pairs") & 1) == 0
    keeps_first = kept_slot() == 0
    mine, other = mine_ref[...], other_ref[...]
    sources = (((second_come, first_come), (first_ref, second_ref)), ((second_ref, first_ref), (first_come, second_come)))
    slots = [jnp.where(keeps_first, mine, other), jnp.where(keeps_first, other, mine)]
    for slot in range(2):
        for half in range(2):
            at = 2 * half + slot
            power[:, at * BLOCK : (at + 1) * BLOCK] = slots[slot][NORMS + half : NORMS + half + 1]
    copies = [pltpu.make_async_copy(power, power_hbm, sems.at[4])]
    copies[0].start()
    for slot, angles in enumerate(slots):
        lags = Lags(offsets, slot)
        blocks = [slice(at * BLOCK, (at + 1) * BLOCK) for at in (slot, 2 + slot)]
        turns = [angles[index : index + 1] for index in range(NORMS)]
        for start in range(0, rows, BATCH):
            span = slice(start, start + BATCH)
            x, y = [
                [jnp.where(is_even, a, b) for a, b in zip(halves(even_ref, span), halves(odd_ref, span))]
                for even_ref, odd_ref in sources[slot]
            ]
            upper = block_after(x, turns[:4], lags.gap)
            lower = left(block_after(y, turns[4:8], lags.gap), lags.lag)
            upper, lower = turn(upper, lower, turns[8], turns[9])
            upper, lower = turn(upper, left(lower, lags.turn), turns[10], turns[11])
            rotated[span, blocks[0]] = right(upper, lags.x_shift) if slot else upper
            rotated[span, blocks[1]] = right(lower, lags.out)
        for half, columns in enumerate(blocks):
            copies.append(pltpu.make_async_copy(rotated.at[:, columns], rotated_hbm.at[:, columns], sems.at[2 * slot + half]))
            copies[-1].start()
    for copy in copies:
        copy.wait()


VMEM = pl.BlockSpec(memory_space=pltpu.VMEM)
HBM = pl.BlockSpec(memory_space=pltpu.HBM)


def call(kernel, operands, outs, name, scratch=(), micros=1, grant=VMEM_LIMIT):
    return pl.pallas_call(
        kernel,
        out_shape=[jax.ShapeDtypeStruct(shape, jnp.float32) for shape, _ in outs],
        in_specs=[space for _, space in operands],
        out_specs=[space for _, space in outs],
        scratch_shapes=scratch,
        name=name,
        cost_estimate=pl.CostEstimate(flops=micros * 10**9, bytes_accessed=micros * 10**6, transcendentals=0),
        compiler_params=pltpu.CompilerParams(vmem_limit_bytes=grant),
    )(*[array for array, _ in operands])


def swap_rows(x, partner):
    size = lax.axis_size("rows")
    depth = size // 4

    def other(row):
        y, z, core = partner(row // (2 * depth), (row // 2) % depth, row % 2)
        return (y * depth + z) * 2 + core

    return lax.ppermute(x, "rows", [(row, other(row)) for row in range(size)])


OPPOSITE = (6, 7, 4, 5, 2, 3, 0, 1)


def per_device(loads, col_weights, partner_offsets, skip_mask):
    rows, columns = loads.shape
    pairs = lax.axis_size("pairs")
    weights = (col_weights.reshape(1, columns), VMEM)
    offsets, skips = (partner_offsets, VMEM), (skip_mask, VMEM)
    is_even = (lax.axis_index("pairs") & 1) == 0
    blocks = [loads[:, at * BLOCK : (at + 1) * BLOCK] for at in range(4)]
    raw = [
        jnp.concatenate([jnp.where(is_even, blocks[even + at], blocks[1 - even + at]) for at in (0, 2)], axis=1) for even in (1, 0)
    ]

    def swap_first(x):
        return lax.ppermute(x, "pairs", [(at, at ^ 1) for at in range(pairs)])

    def swap_second(x):
        size = lax.axis_size("rows")

        def other(row, at):
            to = (row, ((at + 1) ^ 1) - 1) if 0 < at < pairs - 1 else (row ^ 1, at)
            return to[0] * pairs + to[1]

        places = [(row, at) for row in range(size) for at in range(pairs)]
        return lax.ppermute(x, ("rows", "pairs"), [(row * pairs + at, other(row, at)) for row, at in places])

    pair, side = ((rows, 2 * BLOCK), VMEM), ((SIDE, BLOCK), VMEM)
    second_raw = swap_second(raw[1])
    first_raw = swap_first(raw[0])
    first, second, first_side, second_side = [
        (array, VMEM)
        for array in call(own_kernel, [offsets, skips, weights] + [(array, VMEM) for array in raw], [pair, pair, side, side], "own")
    ]
    slots, come = [], []
    for odd_slot, own, own_side, raw_come, side_come in (
        (1, first, first_side, second_raw, swap_second(second_side[0])),
        (0, second, second_side, first_raw, swap_first(first_side[0])),
    ):
        sums, aligned = call(
            functools.partial(cross_kernel, odd_slot),
            [offsets, skips, own, own_side, (raw_come, VMEM), (side_come, VMEM), second, second_side, (slots[-1] if slots else second_side[0], VMEM)],
            [((SUMS, BLOCK), VMEM), pair],
            "cross",
            [pltpu.VMEM((rows, 6 * BLOCK), jnp.float32)],
        )
        slots.append(sums)
        come.append((aligned, VMEM))
    slots, come = slots[::-1], come[::-1]
    keeps_first = (lax.axis_index("pairs") & 1) == kept_slot()
    sums = jnp.where(keeps_first, slots[1], slots[0])
    sums = sums + swap_rows(jnp.where(keeps_first, slots[0], slots[1]), lambda y, z, core: (y, z, 1 - core))
    sums = sums + swap_rows(sums, lambda y, z, core: (1 - y, z, 1 - core))
    near = [swap_rows(sums, lambda y, z, core, by=by: (y, z ^ by, core if by == 3 else 1 - core)) for by in (3, 2, 1)]
    sums = (sums + near[0]) + (near[1] + near[2])
    sums = sums + swap_rows(sums, lambda y, z, core: (y, OPPOSITE[z], 1 - core))
    total_rows = float(rows * lax.axis_size("rows"))
    (angles,) = call(functools.partial(angles_kernel, total_rows), [offsets, (sums, VMEM)], [((ANGLES, BLOCK), VMEM)], "angles")
    other = swap_rows(angles, lambda y, z, core: (y, z, 1 - core))
    rotated, power = call(
        last_kernel,
        [offsets, (angles, VMEM), (other, VMEM), first, second] + come,
        [((rows, columns), HBM), ((1, columns), HBM)],
        "last",
        [pltpu.VMEM((rows, columns), jnp.float32), pltpu.VMEM((1, columns), jnp.float32), pltpu.SemaphoreType.DMA((5,))],
    )
    return rotated, power.reshape(columns)


def solution(mesh):
    in_specs = (P("rows", "pairs"), P("pairs"), P(), P(None, "pairs"))
    out_specs = (P("rows", "pairs"), P("pairs"))
    return jax.shard_map(
        per_device, mesh=mesh, in_specs=in_specs, out_specs=out_specs, check_vma=False
    )
```

```python
import functools
import jax
import jax.numpy as jnp
from jax import lax
from jax.experimental import pallas as pl
from jax.experimental.pallas import tpu as pltpu
from jax.sharding import PartitionSpec as P

BLOCK = 128
GROUP = 8
BATCH = 128
LAST_BATCH = 64

STATS = 19
CROSS = 2 * STATS
FLAGS = CROSS + 36
SUMS = 80
SIDE = 24
NORMS = 12
ANGLES = 16
VMEM_LIMIT = 8 * 1024 * 1024


def left(x, by):
    return pltpu.roll(x, (-by) & (BLOCK - 1), 1)


def right(x, by):
    return pltpu.roll(x, by & (BLOCK - 1), 1)


def at_end():
    place = lax.axis_index("pairs")
    return (place == 0) | (place == lax.axis_size("pairs") - 1)


def kept_slot():
    row = lax.axis_index("rows")
    return (row ^ (row >> 1) ^ (row >> 2) ^ (row >> 4)) & 1


class Lags:
    def __init__(self, offsets, slot):
        place = lax.axis_index("pairs")
        self.first = offsets[0, 0]
        self.gap = offsets[0, 1] - offsets[0, 0]
        self.turn = offsets[1, 1] - offsets[1, 0]
        self.x_low = (slot == 1) & (place == 0)
        self.y_up = (slot == 1) & (place == lax.axis_size("pairs") - 1)
        self.x_shift = jnp.where(self.x_low, offsets[0, 1], 0)
        y_shift = jnp.where(self.y_up, 0, offsets[0, 1])
        self.lag = offsets[1, 0] - y_shift + self.x_shift
        self.out = self.x_shift + offsets[1, 1]

    def crossed(self):
        return (self.lag, self.lag + self.turn, self.lag - self.turn)


def halves(ref, span):
    return ref[span, :BLOCK], ref[span, BLOCK:]


def sums_over(rows, terms):
    totals = None
    for start in range(0, rows, BATCH):
        parts = [jnp.sum(term.reshape(BATCH // GROUP, GROUP, BLOCK), axis=0) for term in terms(slice(start, start + BATCH))]
        totals = parts if totals is None else [total + part for total, part in zip(totals, parts)]
    return [jnp.sum(total, axis=0, keepdims=True) for total in totals]


def store_rows(out_ref, start, values):
    for index, value in enumerate(values):
        out_ref[start + index : start + index + 1, :] = value


def moved_by_gap(x, lags):
    return [left(half, lags.gap) for half in x], x, [right(half, lags.gap) for half in x]


def lagged(x_moved, y, lag):
    ahead = [left(half, lag) for half in y]
    return [a * b for x in x_moved for a in x for b in ahead]


def pair_stats(ref, lags):
    def terms(span):
        pair = halves(ref, span)
        moved = moved_by_gap(pair, lags)
        (upper, lower), (upper_gap, lower_gap) = pair, moved[0]
        step_0 = [upper * upper, lower * lower, upper * lower, upper * lower_gap, upper_gap * lower, upper * upper_gap, lower * lower_gap]
        return step_0 + lagged(moved, pair, lags.turn)

    return sums_over(ref.shape[0], terms)


def angle(first_norms, second_norms, coupling):
    half_gap = 0.5 * (second_norms - first_norms)
    gap_sign = jnp.where(half_gap >= 0.0, 1.0, -1.0)
    denominator = jnp.maximum(
        jnp.abs(half_gap) + jnp.sqrt(half_gap * half_gap + coupling * coupling),
        1e-06 * (first_norms + second_norms),
    )
    tangent = gap_sign * coupling / denominator
    cosine = 1.0 / jnp.sqrt(1.0 + tangent * tangent)
    return cosine, tangent * cosine


def turned_norms(first_norms, second_norms, coupling, cosine, sine):
    new_first = cosine * (cosine * first_norms - sine * coupling) - sine * (cosine * coupling - sine * second_norms)
    new_second = sine * (sine * first_norms + cosine * coupling) + cosine * (sine * coupling + cosine * second_norms)
    return new_first, new_second


def two_rounds(first_norms, second_norms, couplings, gap, keep):
    same, ahead, behind, firsts, seconds = couplings
    cosine, sine = angle(first_norms, second_norms, same)
    new_first, new_second = turned_norms(first_norms, second_norms, same, cosine, sine)
    cosine_gap, sine_gap = left(cosine, gap), left(sine, gap)
    coupling = cosine * (sine_gap * firsts + cosine_gap * ahead) - sine * (sine_gap * behind + cosine_gap * seconds)
    new_second = left(new_second, gap)
    cosine_last, sine_last = angle(new_first, new_second, coupling)
    new_first, new_second = turned_norms(new_first, new_second, coupling, cosine_last, sine_last)
    one, zero = jnp.ones_like(cosine), jnp.zeros_like(cosine)
    turns = (
        jnp.where(keep, one, cosine),
        jnp.where(keep, zero, sine),
        jnp.where(keep, one, cosine_last),
        jnp.where(keep, zero, sine_last),
    )
    return turns, (jnp.where(keep, first_norms, new_first), jnp.where(keep, left(second_norms, gap), new_second))


def joint(x_weights, y_weights, dots, gap):
    total = None
    for a in range(2):
        for b in range(2):
            (x_here, x_gap), (y_here, y_gap) = x_weights[a], y_weights[b]
            before, at, after = [dots[4 * index + 2 * a + b] for index in range(3)]
            part = x_here * (y_here * at + y_gap * left(after, gap)) + x_gap * (y_here * before + y_gap * left(at, gap))
            total = part if total is None else total + part
    return total


def rolled(weights, by):
    return [[left(value, by) for value in pair] for pair in weights]


def align_into(out_ref, raw, weights, lags):
    for start in range(0, out_ref.shape[0], BATCH):
        span = slice(start, start + BATCH)
        upper, lower = raw(span)
        out_ref[span, :BLOCK] = upper * weights[0]
        out_ref[span, BLOCK:] = left(lower, lags.first) * weights[1]


def own_kernel(offsets, skip, weights_ref, first_raw, second_raw, first_ref, second_ref, first_side, second_side):
    lags = Lags(offsets, 0)
    is_even = (lax.axis_index("pairs") & 1) == 0
    weights = [weights_ref[:, block * BLOCK : (block + 1) * BLOCK] for block in range(4)]
    skips = [skip[0, pair].astype(jnp.float32) for pair in range(2)]
    for even, raw_ref, ref, side in ((1, first_raw, first_ref, first_side), (0, second_raw, second_ref, second_side)):
        odd = 1 - even
        weight = [jnp.where(is_even, weights[2 * half + even], weights[2 * half + odd]) for half in range(2)]
        weight[1] = left(weight[1], lags.first)
        align_into(ref, functools.partial(halves, raw_ref), weight, lags)
        flag = jnp.full((1, BLOCK), jnp.where(is_even, skips[even], skips[odd]), jnp.float32)
        rows = pair_stats(ref, lags) + weight + [flag]
        store_rows(side, 0, rows + [jnp.zeros_like(flag)] * (SIDE - len(rows)))


def cross_kernel(odd_slot, offsets, skip, own_ref, own_side, raw_ref, come_side, end_ref, end_side, _, out_ref, come_ref, moved_ref):
    is_even = (lax.axis_index("pairs") & 1) == 0
    slot = jnp.where(is_even, 1 - odd_slot, odd_slot)
    lags = Lags(offsets, slot)
    own_first = slot == 1
    rows = range(STATS + 3)
    own = [own_side[row : row + 1, :] for row in rows]
    come = [come_side[row : row + 1, :] for row in rows]
    align_into(come_ref, functools.partial(halves, raw_ref), come[STATS : STATS + 2], lags)
    if odd_slot == 1:

        @pl.when(at_end())
        def _():
            come_ref[...] = end_ref[...]

        come = [jnp.where(at_end(), end_side[row : row + 1, :], value) for row, value in zip(rows, come)]
    step_flag = jnp.full((1, BLOCK), jnp.where(own_first, skip[1, 1], skip[1, 0]).astype(jnp.float32), jnp.float32)

    def pick(mine, theirs):
        return [jnp.where(own_first, a, b) for a, b in zip(mine, theirs)], [jnp.where(own_first, b, a) for a, b in zip(mine, theirs)]

    x_side, y_side = pick(own, come)
    store_rows(out_ref, 0, x_side[:STATS] + y_side[:STATS])
    for start in range(0, own_ref.shape[0], BATCH):
        span = slice(start, start + BATCH)
        x, _ = pick(halves(own_ref, span), halves(come_ref, span))
        for at, half in enumerate(half for pair in moved_by_gap(x, lags) for half in pair):
            moved_ref[span, at * BLOCK : (at + 1) * BLOCK] = half
    for index, lag in enumerate(lags.crossed()):

        def terms(span):
            _, y = pick(halves(own_ref, span), halves(come_ref, span))
            moved = [[moved_ref[span, at * BLOCK : (at + 1) * BLOCK] for at in (two, two + 1)] for two in (0, 2, 4)]
            return lagged(moved, y, lag)

        store_rows(out_ref, CROSS + 12 * index, sums_over(own_ref.shape[0], terms))
    store_rows(out_ref, FLAGS, x_side[-1:] + y_side[-1:] + [step_flag] + [jnp.zeros_like(step_flag)] * (SUMS - FLAGS - 3))


def angles_kernel(total_rows, offsets, sums_ref, out_ref):
    lags = Lags(offsets, kept_slot())
    rows = [sums_ref[index : index + 1, :] for index in range(FLAGS + 3)]
    sides = []
    for side, is_low in ((0, lags.x_low), (1, jnp.logical_not(lags.y_up))):
        stats = rows[side * STATS : (side + 1) * STATS]
        (cosine, sine, cosine_last, sine_last), norms = two_rounds(stats[0], stats[1], stats[2:7], lags.gap, rows[FLAGS + side] > 0.5)
        here = jnp.where(is_low, sine_last, cosine_last)
        ahead = jnp.where(is_low, cosine_last, -sine_last)
        weights = [
            [here * cosine, ahead * left(sine, lags.gap)],
            [-here * sine, ahead * left(cosine, lags.gap)],
        ]
        sides.append((jnp.where(is_low, norms[1], norms[0]), weights, stats[7:], [cosine, sine, here, ahead]))
    (x_norms, x_weights, x_dots, x_turns), (y_norms, y_weights, y_dots, y_turns) = sides
    crossed = [
        joint(x_weights, rolled(y_weights, lag), rows[CROSS + 12 * index : CROSS + 12 * (index + 1)], lags.gap)
        for index, lag in enumerate(lags.crossed())
    ]
    firsts = joint(x_weights, rolled(x_weights, lags.turn), x_dots, lags.gap)
    seconds = left(joint(y_weights, rolled(y_weights, lags.turn), y_dots, lags.gap), lags.lag)
    couplings = (crossed[0], crossed[1], left(crossed[2], lags.turn), firsts, seconds)
    turns, (upper, lower) = two_rounds(x_norms, left(y_norms, lags.lag), couplings, lags.turn, rows[FLAGS + 2] > 0.5)
    norms = [right(upper, lags.x_shift) / total_rows, right(lower, lags.out) / total_rows]
    store_rows(out_ref, 0, x_turns + y_turns + list(turns) + norms + [jnp.zeros_like(upper)] * (ANGLES - NORMS - 2))


def turn(x, y, cosine, sine):
    return cosine * x - sine * y, sine * x + cosine * y


def block_after(pair, turns, gap):
    cosine, sine, here, ahead = turns
    upper, lower = turn(*pair, cosine, sine)
    return here * upper + ahead * left(lower, gap)


def last_kernel(offsets, mine_ref, other_ref, first_ref, second_ref, first_come, second_come,
                rotated_hbm, power_hbm, rotated, power, sems):
    rows = rotated.shape[0]
    is_even = (lax.axis_index("pairs") & 1) == 0
    keeps_first = kept_slot() == 0
    mine, other = mine_ref[...], other_ref[...]
    sources = (((second_come, first_come), (first_ref, second_ref)), ((second_ref, first_ref), (first_come, second_come)))
    slots = [jnp.where(keeps_first, mine, other), jnp.where(keeps_first, other, mine)]
    for slot in range(2):
        for half in range(2):
            at = 2 * half + slot
            power[:, at * BLOCK : (at + 1) * BLOCK] = slots[slot][NORMS + half : NORMS + half + 1]
    copies = [pltpu.make_async_copy(power, power_hbm, sems.at[4])]
    copies[0].start()
    for slot, angles in enumerate(slots):
        lags = Lags(offsets, slot)
        blocks = [slice(at * BLOCK, (at + 1) * BLOCK) for at in (slot, 2 + slot)]
        turns = [angles[index : index + 1] for index in range(NORMS)]
        for start in range(0, rows, LAST_BATCH):
            span = slice(start, start + LAST_BATCH)
            x, y = [
                [jnp.where(is_even, a, b) for a, b in zip(halves(even_ref, span), halves(odd_ref, span))]
                for even_ref, odd_ref in sources[slot]
            ]
            upper = block_after(x, turns[:4], lags.gap)
            lower = left(block_after(y, turns[4:8], lags.gap), lags.lag)
            upper, lower = turn(upper, lower, turns[8], turns[9])
            upper, lower = turn(upper, left(lower, lags.turn), turns[10], turns[11])
            rotated[span, blocks[0]] = right(upper, lags.x_shift) if slot else upper
            rotated[span, blocks[1]] = right(lower, lags.out)
        for half, columns in enumerate(blocks):
            copies.append(pltpu.make_async_copy(rotated.at[:, columns], rotated_hbm.at[:, columns], sems.at[2 * slot + half]))
            copies[-1].start()
    for copy in copies:
        copy.wait()


VMEM = pl.BlockSpec(memory_space=pltpu.VMEM)
HBM = pl.BlockSpec(memory_space=pltpu.HBM)


def call(kernel, operands, outs, name, scratch=(), micros=1, grant=VMEM_LIMIT):
    return pl.pallas_call(
        kernel,
        out_shape=[jax.ShapeDtypeStruct(shape, jnp.float32) for shape, _ in outs],
        in_specs=[space for _, space in operands],
        out_specs=[space for _, space in outs],
        scratch_shapes=scratch,
        name=name,
        cost_estimate=pl.CostEstimate(flops=micros * 10**9, bytes_accessed=micros * 10**6, transcendentals=0),
        compiler_params=pltpu.CompilerParams(vmem_limit_bytes=grant),
    )(*[array for array, _ in operands])


def swap_rows(x, partner):
    size = lax.axis_size("rows")
    depth = size // 4

    def other(row):
        y, z, core = partner(row // (2 * depth), (row // 2) % depth, row % 2)
        return (y * depth + z) * 2 + core

    return lax.ppermute(x, "rows", [(row, other(row)) for row in range(size)])


OPPOSITE = (6, 7, 4, 5, 2, 3, 0, 1)


def per_device(loads, col_weights, partner_offsets, skip_mask):
    rows, columns = loads.shape
    pairs = lax.axis_size("pairs")
    weights = (col_weights.reshape(1, columns), VMEM)
    offsets, skips = (partner_offsets, VMEM), (skip_mask, VMEM)
    is_even = (lax.axis_index("pairs") & 1) == 0

    def selected(even):
        at = jnp.where(is_even, even, 1 - even) * BLOCK
        return jnp.concatenate([lax.dynamic_slice(loads, (0, at + half * 2 * BLOCK), (rows, BLOCK)) for half in range(2)], axis=1)

    raw = [selected(1), selected(0)]

    def swap_first(x):
        return lax.ppermute(x, "pairs", [(at, at ^ 1) for at in range(pairs)])

    def swap_second(x):
        size = lax.axis_size("rows")

        def other(row, at):
            to = (row, ((at + 1) ^ 1) - 1) if 0 < at < pairs - 1 else (row ^ 1, at)
            return to[0] * pairs + to[1]

        places = [(row, at) for row in range(size) for at in range(pairs)]
        return lax.ppermute(x, ("rows", "pairs"), [(row * pairs + at, other(row, at)) for row, at in places])

    pair, side = ((rows, 2 * BLOCK), VMEM), ((SIDE, BLOCK), VMEM)
    second_raw = swap_second(raw[1])
    first_raw = swap_first(raw[0])
    first, second, first_side, second_side = [
        (array, VMEM)
        for array in call(own_kernel, [offsets, skips, weights] + [(array, VMEM) for array in raw], [pair, pair, side, side], "own")
    ]
    slots, come = [], []
    for odd_slot, own, own_side, raw_come, side_come in (
        (1, first, first_side, second_raw, swap_second(second_side[0])),
        (0, second, second_side, first_raw, swap_first(first_side[0])),
    ):
        sums, aligned = call(
            functools.partial(cross_kernel, odd_slot),
            [offsets, skips, own, own_side, (raw_come, VMEM), (side_come, VMEM), second, second_side, (slots[-1] if slots else second_side[0], VMEM)],
            [((SUMS, BLOCK), VMEM), pair],
            "cross",
            [pltpu.VMEM((rows, 6 * BLOCK), jnp.float32)],
        )
        slots.append(sums)
        come.append((aligned, VMEM))
    slots, come = slots[::-1], come[::-1]
    keeps_first = (lax.axis_index("pairs") & 1) == kept_slot()
    sums = jnp.where(keeps_first, slots[1], slots[0])
    sums = sums + swap_rows(jnp.where(keeps_first, slots[0], slots[1]), lambda y, z, core: (y, z, 1 - core))
    sums = sums + swap_rows(sums, lambda y, z, core: (1 - y, z, 1 - core))
    near = [swap_rows(sums, lambda y, z, core, by=by: (y, z ^ by, core if by == 3 else 1 - core)) for by in (3, 2, 1)]
    sums = (sums + near[0]) + (near[1] + near[2])
    sums = sums + swap_rows(sums, lambda y, z, core: (y, OPPOSITE[z], 1 - core))
    total_rows = float(rows * lax.axis_size("rows"))
    (angles,) = call(functools.partial(angles_kernel, total_rows), [offsets, (sums, VMEM)], [((ANGLES, BLOCK), VMEM)], "angles")
    other = swap_rows(angles, lambda y, z, core: (y, z, 1 - core))
    rotated, power = call(
        last_kernel,
        [offsets, (angles, VMEM), (other, VMEM), first, second] + come,
        [((rows, columns), HBM), ((1, columns), HBM)],
        "last",
        [pltpu.VMEM((rows, columns), jnp.float32), pltpu.VMEM((1, columns), jnp.float32), pltpu.SemaphoreType.DMA((5,))],
    )
    return rotated, power.reshape(columns)


def solution(mesh):
    in_specs = (P("rows", "pairs"), P("pairs"), P(), P(None, "pairs"))
    out_specs = (P("rows", "pairs"), P("pairs"))
    return jax.shard_map(
        per_device, mesh=mesh, in_specs=in_specs, out_specs=out_specs, check_vma=False
    )
```

```python
import functools
import jax
import jax.numpy as jnp
from jax import lax
from jax.experimental import pallas as pl
from jax.experimental.pallas import tpu as pltpu
from jax.sharding import PartitionSpec as P

BLOCK = 128
GROUP = 8
BATCH = 128
LAST_BATCH = 64

STATS = 19
CROSS = 2 * STATS
FLAGS = CROSS + 36
SUMS = 80
SIDE = 24
NORMS = 12
ANGLES = 16
VMEM_LIMIT = 8 * 1024 * 1024


def left(x, by):
    return pltpu.roll(x, (-by) & (BLOCK - 1), 1)


def right(x, by):
    return pltpu.roll(x, by & (BLOCK - 1), 1)


def at_end():
    place = lax.axis_index("pairs")
    return (place == 0) | (place == lax.axis_size("pairs") - 1)


def kept_slot():
    row = lax.axis_index("rows")
    return (row ^ (row >> 1) ^ (row >> 2) ^ (row >> 4)) & 1


class Lags:
    def __init__(self, offsets, slot):
        place = lax.axis_index("pairs")
        self.first = offsets[0, 0]
        self.gap = offsets[0, 1] - offsets[0, 0]
        self.turn = offsets[1, 1] - offsets[1, 0]
        self.x_low = (slot == 1) & (place == 0)
        self.y_up = (slot == 1) & (place == lax.axis_size("pairs") - 1)
        self.x_shift = jnp.where(self.x_low, offsets[0, 1], 0)
        y_shift = jnp.where(self.y_up, 0, offsets[0, 1])
        self.lag = offsets[1, 0] - y_shift + self.x_shift
        self.out = self.x_shift + offsets[1, 1]

    def crossed(self):
        return (self.lag, self.lag + self.turn, self.lag - self.turn)


def halves(ref, span):
    return ref[span, :BLOCK], ref[span, BLOCK:]


def sums_over(rows, terms):
    totals = None
    for start in range(0, rows, BATCH):
        parts = [jnp.sum(term.reshape(BATCH // GROUP, GROUP, BLOCK), axis=0) for term in terms(slice(start, start + BATCH))]
        totals = parts if totals is None else [total + part for total, part in zip(totals, parts)]
    return [jnp.sum(total, axis=0, keepdims=True) for total in totals]


def store_rows(out_ref, start, values):
    for index, value in enumerate(values):
        out_ref[start + index : start + index + 1, :] = value


def moved_by_gap(x, lags):
    return [left(half, lags.gap) for half in x], x, [right(half, lags.gap) for half in x]


def lagged(x_moved, y, lag):
    ahead = [left(half, lag) for half in y]
    return [a * b for x in x_moved for a in x for b in ahead]


def pair_stats(ref, lags):
    def terms(span):
        pair = halves(ref, span)
        moved = moved_by_gap(pair, lags)
        (upper, lower), (upper_gap, lower_gap) = pair, moved[0]
        step_0 = [upper * upper, lower * lower, upper * lower, upper * lower_gap, upper_gap * lower, upper * upper_gap, lower * lower_gap]
        return step_0 + lagged(moved, pair, lags.turn)

    return sums_over(ref.shape[0], terms)


def angle(first_norms, second_norms, coupling):
    half_gap = 0.5 * (second_norms - first_norms)
    gap_sign = jnp.where(half_gap >= 0.0, 1.0, -1.0)
    denominator = jnp.maximum(
        jnp.abs(half_gap) + jnp.sqrt(half_gap * half_gap + coupling * coupling),
        1e-06 * (first_norms + second_norms),
    )
    tangent = gap_sign * coupling / denominator
    cosine = lax.rsqrt(1.0 + tangent * tangent)
    return cosine, tangent * cosine


def turned_norms(first_norms, second_norms, coupling, cosine, sine):
    new_first = cosine * (cosine * first_norms - sine * coupling) - sine * (cosine * coupling - sine * second_norms)
    new_second = sine * (sine * first_norms + cosine * coupling) + cosine * (sine * coupling + cosine * second_norms)
    return new_first, new_second


def two_rounds(first_norms, second_norms, couplings, gap, keep):
    same, ahead, behind, firsts, seconds = couplings
    cosine, sine = angle(first_norms, second_norms, same)
    new_first, new_second = turned_norms(first_norms, second_norms, same, cosine, sine)
    cosine_gap, sine_gap = left(cosine, gap), left(sine, gap)
    coupling = cosine * (sine_gap * firsts + cosine_gap * ahead) - sine * (sine_gap * behind + cosine_gap * seconds)
    new_second = left(new_second, gap)
    cosine_last, sine_last = angle(new_first, new_second, coupling)
    new_first, new_second = turned_norms(new_first, new_second, coupling, cosine_last, sine_last)
    one, zero = jnp.ones_like(cosine), jnp.zeros_like(cosine)
    turns = (
        jnp.where(keep, one, cosine),
        jnp.where(keep, zero, sine),
        jnp.where(keep, one, cosine_last),
        jnp.where(keep, zero, sine_last),
    )
    return turns, (jnp.where(keep, first_norms, new_first), jnp.where(keep, left(second_norms, gap), new_second))


def joint(x_weights, y_weights, dots, gap):
    total = None
    for a in range(2):
        for b in range(2):
            (x_here, x_gap), (y_here, y_gap) = x_weights[a], y_weights[b]
            before, at, after = [dots[4 * index + 2 * a + b] for index in range(3)]
            part = x_here * (y_here * at + y_gap * left(after, gap)) + x_gap * (y_here * before + y_gap * left(at, gap))
            total = part if total is None else total + part
    return total


def rolled(weights, by):
    return [[left(value, by) for value in pair] for pair in weights]


def align_into(out_ref, raw, weights, lags):
    for start in range(0, out_ref.shape[0], BATCH):
        span = slice(start, start + BATCH)
        upper, lower = raw(span)
        out_ref[span, :BLOCK] = upper * weights[0]
        out_ref[span, BLOCK:] = left(lower, lags.first) * weights[1]


def own_kernel(offsets, skip, weights_ref, first_raw, second_raw, first_ref, second_ref, first_side, second_side):
    lags = Lags(offsets, 0)
    is_even = (lax.axis_index("pairs") & 1) == 0
    weights = [weights_ref[:, block * BLOCK : (block + 1) * BLOCK] for block in range(4)]
    skips = [skip[0, pair].astype(jnp.float32) for pair in range(2)]
    for even, raw_ref, ref, side in ((1, first_raw, first_ref, first_side), (0, second_raw, second_ref, second_side)):
        odd = 1 - even
        weight = [jnp.where(is_even, weights[2 * half + even], weights[2 * half + odd]) for half in range(2)]
        weight[1] = left(weight[1], lags.first)
        align_into(ref, functools.partial(halves, raw_ref), weight, lags)
        flag = jnp.full((1, BLOCK), jnp.where(is_even, skips[even], skips[odd]), jnp.float32)
        rows = pair_stats(ref, lags) + weight + [flag]
        store_rows(side, 0, rows + [jnp.zeros_like(flag)] * (SIDE - len(rows)))


def cross_kernel(odd_slot, offsets, skip, own_ref, own_side, raw_ref, come_side, end_ref, end_side, _, out_ref, come_ref, moved_ref):
    is_even = (lax.axis_index("pairs") & 1) == 0
    slot = jnp.where(is_even, 1 - odd_slot, odd_slot)
    lags = Lags(offsets, slot)
    own_first = slot == 1
    rows = range(STATS + 3)
    own = [own_side[row : row + 1, :] for row in rows]
    come = [come_side[row : row + 1, :] for row in rows]
    align_into(come_ref, functools.partial(halves, raw_ref), come[STATS : STATS + 2], lags)
    if odd_slot == 1:

        @pl.when(at_end())
        def _():
            come_ref[...] = end_ref[...]

        come = [jnp.where(at_end(), end_side[row : row + 1, :], value) for row, value in zip(rows, come)]
    step_flag = jnp.full((1, BLOCK), jnp.where(own_first, skip[1, 1], skip[1, 0]).astype(jnp.float32), jnp.float32)

    def pick(mine, theirs):
        return [jnp.where(own_first, a, b) for a, b in zip(mine, theirs)], [jnp.where(own_first, b, a) for a, b in zip(mine, theirs)]

    x_side, y_side = pick(own, come)
    store_rows(out_ref, 0, x_side[:STATS] + y_side[:STATS])
    for start in range(0, own_ref.shape[0], BATCH):
        span = slice(start, start + BATCH)
        x, _ = pick(halves(own_ref, span), halves(come_ref, span))
        for at, half in enumerate(half for pair in moved_by_gap(x, lags) for half in pair):
            moved_ref[span, at * BLOCK : (at + 1) * BLOCK] = half
    for index, lag in enumerate(lags.crossed()):

        def terms(span):
            _, y = pick(halves(own_ref, span), halves(come_ref, span))
            moved = [[moved_ref[span, at * BLOCK : (at + 1) * BLOCK] for at in (two, two + 1)] for two in (0, 2, 4)]
            return lagged(moved, y, lag)

        store_rows(out_ref, CROSS + 12 * index, sums_over(own_ref.shape[0], terms))
    store_rows(out_ref, FLAGS, x_side[-1:] + y_side[-1:] + [step_flag] + [jnp.zeros_like(step_flag)] * (SUMS - FLAGS - 3))


def angles_kernel(total_rows, offsets, sums_ref, out_ref):
    lags = Lags(offsets, kept_slot())
    rows = [sums_ref[index : index + 1, :] for index in range(FLAGS + 3)]
    sides = []
    for side, is_low in ((0, lags.x_low), (1, jnp.logical_not(lags.y_up))):
        stats = rows[side * STATS : (side + 1) * STATS]
        (cosine, sine, cosine_last, sine_last), norms = two_rounds(stats[0], stats[1], stats[2:7], lags.gap, rows[FLAGS + side] > 0.5)
        here = jnp.where(is_low, sine_last, cosine_last)
        ahead = jnp.where(is_low, cosine_last, -sine_last)
        weights = [
            [here * cosine, ahead * left(sine, lags.gap)],
            [-here * sine, ahead * left(cosine, lags.gap)],
        ]
        sides.append((jnp.where(is_low, norms[1], norms[0]), weights, stats[7:], [cosine, sine, here, ahead]))
    (x_norms, x_weights, x_dots, x_turns), (y_norms, y_weights, y_dots, y_turns) = sides
    crossed = [
        joint(x_weights, rolled(y_weights, lag), rows[CROSS + 12 * index : CROSS + 12 * (index + 1)], lags.gap)
        for index, lag in enumerate(lags.crossed())
    ]
    firsts = joint(x_weights, rolled(x_weights, lags.turn), x_dots, lags.gap)
    seconds = left(joint(y_weights, rolled(y_weights, lags.turn), y_dots, lags.gap), lags.lag)
    couplings = (crossed[0], crossed[1], left(crossed[2], lags.turn), firsts, seconds)
    turns, (upper, lower) = two_rounds(x_norms, left(y_norms, lags.lag), couplings, lags.turn, rows[FLAGS + 2] > 0.5)
    norms = [right(upper, lags.x_shift) / total_rows, right(lower, lags.out) / total_rows]
    store_rows(out_ref, 0, x_turns + y_turns + list(turns) + norms + [jnp.zeros_like(upper)] * (ANGLES - NORMS - 2))


def turn(x, y, cosine, sine):
    return cosine * x - sine * y, sine * x + cosine * y


def block_after(pair, turns, gap):
    cosine, sine, here, ahead = turns
    upper, lower = turn(*pair, cosine, sine)
    return here * upper + ahead * left(lower, gap)


def last_kernel(offsets, mine_ref, other_ref, first_ref, second_ref, first_come, second_come,
                rotated_hbm, power_hbm, rotated, power, sems):
    rows = rotated.shape[0]
    is_even = (lax.axis_index("pairs") & 1) == 0
    keeps_first = kept_slot() == 0
    mine, other = mine_ref[...], other_ref[...]
    sources = (((second_come, first_come), (first_ref, second_ref)), ((second_ref, first_ref), (first_come, second_come)))
    slots = [jnp.where(keeps_first, mine, other), jnp.where(keeps_first, other, mine)]
    for slot in range(2):
        for half in range(2):
            at = 2 * half + slot
            power[:, at * BLOCK : (at + 1) * BLOCK] = slots[slot][NORMS + half : NORMS + half + 1]
    copies = [pltpu.make_async_copy(power, power_hbm, sems.at[4])]
    copies[0].start()
    for slot, angles in enumerate(slots):
        lags = Lags(offsets, slot)
        blocks = [slice(at * BLOCK, (at + 1) * BLOCK) for at in (slot, 2 + slot)]
        turns = [angles[index : index + 1] for index in range(NORMS)]
        for start in range(0, rows, LAST_BATCH):
            span = slice(start, start + LAST_BATCH)
            x, y = [
                [jnp.where(is_even, a, b) for a, b in zip(halves(even_ref, span), halves(odd_ref, span))]
                for even_ref, odd_ref in sources[slot]
            ]
            upper = block_after(x, turns[:4], lags.gap)
            lower = left(block_after(y, turns[4:8], lags.gap), lags.lag)
            upper, lower = turn(upper, lower, turns[8], turns[9])
            upper, lower = turn(upper, left(lower, lags.turn), turns[10], turns[11])
            rotated[span, blocks[0]] = right(upper, lags.x_shift) if slot else upper
            rotated[span, blocks[1]] = right(lower, lags.out)
        for half, columns in enumerate(blocks):
            copies.append(pltpu.make_async_copy(rotated.at[:, columns], rotated_hbm.at[:, columns], sems.at[2 * slot + half]))
            copies[-1].start()
    for copy in copies:
        copy.wait()


VMEM = pl.BlockSpec(memory_space=pltpu.VMEM)
HBM = pl.BlockSpec(memory_space=pltpu.HBM)


def call(kernel, operands, outs, name, scratch=(), micros=1, grant=VMEM_LIMIT):
    return pl.pallas_call(
        kernel,
        out_shape=[jax.ShapeDtypeStruct(shape, jnp.float32) for shape, _ in outs],
        in_specs=[space for _, space in operands],
        out_specs=[space for _, space in outs],
        scratch_shapes=scratch,
        name=name,
        cost_estimate=pl.CostEstimate(flops=micros * 10**9, bytes_accessed=micros * 10**6, transcendentals=0),
        compiler_params=pltpu.CompilerParams(vmem_limit_bytes=grant),
    )(*[array for array, _ in operands])


def swap_rows(x, partner):
    size = lax.axis_size("rows")
    depth = size // 4

    def other(row):
        y, z, core = partner(row // (2 * depth), (row // 2) % depth, row % 2)
        return (y * depth + z) * 2 + core

    return lax.ppermute(x, "rows", [(row, other(row)) for row in range(size)])


OPPOSITE = (6, 7, 4, 5, 2, 3, 0, 1)


def per_device(loads, col_weights, partner_offsets, skip_mask):
    rows, columns = loads.shape
    pairs = lax.axis_size("pairs")
    weights = (col_weights.reshape(1, columns), VMEM)
    offsets, skips = (partner_offsets, VMEM), (skip_mask, VMEM)
    is_even = (lax.axis_index("pairs") & 1) == 0

    def selected(even):
        at = jnp.where(is_even, even, 1 - even) * BLOCK
        return jnp.concatenate([lax.dynamic_slice(loads, (0, at + half * 2 * BLOCK), (rows, BLOCK)) for half in range(2)], axis=1)

    raw = [selected(1), selected(0)]

    def swap_first(x):
        return lax.ppermute(x, "pairs", [(at, at ^ 1) for at in range(pairs)])

    def swap_second(x):
        size = lax.axis_size("rows")

        def other(row, at):
            to = (row, ((at + 1) ^ 1) - 1) if 0 < at < pairs - 1 else (row ^ 1, at)
            return to[0] * pairs + to[1]

        places = [(row, at) for row in range(size) for at in range(pairs)]
        return lax.ppermute(x, ("rows", "pairs"), [(row * pairs + at, other(row, at)) for row, at in places])

    pair, side = ((rows, 2 * BLOCK), VMEM), ((SIDE, BLOCK), VMEM)
    second_raw = swap_second(raw[1])
    first_raw = swap_first(raw[0])
    first, second, first_side, second_side = [
        (array, VMEM)
        for array in call(own_kernel, [offsets, skips, weights] + [(array, VMEM) for array in raw], [pair, pair, side, side], "own")
    ]
    slots, come = [], []
    for odd_slot, own, own_side, raw_come, side_come in (
        (1, first, first_side, second_raw, swap_second(second_side[0])),
        (0, second, second_side, first_raw, swap_first(first_side[0])),
    ):
        sums, aligned = call(
            functools.partial(cross_kernel, odd_slot),
            [offsets, skips, own, own_side, (raw_come, VMEM), (side_come, VMEM), second, second_side, (slots[-1] if slots else second_side[0], VMEM)],
            [((SUMS, BLOCK), VMEM), pair],
            "cross",
            [pltpu.VMEM((rows, 6 * BLOCK), jnp.float32)],
        )
        slots.append(sums)
        come.append((aligned, VMEM))
    slots, come = slots[::-1], come[::-1]
    keeps_first = (lax.axis_index("pairs") & 1) == kept_slot()
    sums = jnp.where(keeps_first, slots[1], slots[0])
    sums = sums + swap_rows(jnp.where(keeps_first, slots[0], slots[1]), lambda y, z, core: (y, z, 1 - core))
    sums = sums + swap_rows(sums, lambda y, z, core: (1 - y, z, 1 - core))
    near = [swap_rows(sums, lambda y, z, core, by=by: (y, z ^ by, core if by == 3 else 1 - core)) for by in (3, 2, 1)]
    sums = (sums + near[0]) + (near[1] + near[2])
    sums = sums + swap_rows(sums, lambda y, z, core: (y, OPPOSITE[z], 1 - core))
    total_rows = float(rows * lax.axis_size("rows"))
    (angles,) = call(functools.partial(angles_kernel, total_rows), [offsets, (sums, VMEM)], [((ANGLES, BLOCK), VMEM)], "angles")
    other = swap_rows(angles, lambda y, z, core: (y, z, 1 - core))
    rotated, power = call(
        last_kernel,
        [offsets, (angles, VMEM), (other, VMEM), first, second] + come,
        [((rows, columns), HBM), ((1, columns), HBM)],
        "last",
        [pltpu.VMEM((rows, columns), jnp.float32), pltpu.VMEM((1, columns), jnp.float32), pltpu.SemaphoreType.DMA((5,))],
    )
    return rotated, power.reshape(columns)


def solution(mesh):
    in_specs = (P("rows", "pairs"), P("pairs"), P(), P(None, "pairs"))
    out_specs = (P("rows", "pairs"), P("pairs"))
    return jax.shard_map(
        per_device, mesh=mesh, in_specs=in_specs, out_specs=out_specs, check_vma=False
    )
```
